32 devices in a mesh: dp: 2 (over core), row: 4 (over y, x), col: 4 (over z).
Axes of the slice: x: 2, y: 2, z: 4, core: 2. Of those that a mesh axis runs over, the one named last changes fastest.
Arguments:
- hidden_in: bfloat16 [32, 768, 1024], P(('dp', 'col'), 'row'), may hold values from -6 to 6
- lengths: int32 [32], P(('dp', 'col')), may hold values from 256 to 1024, as said below
- w_qkv: bfloat16 [768, 3, 768], P('col', None, 'row'), may hold values from -0.21875 to 0.21875
- w_out: bfloat16 [768, 768], P('row', 'col'), may hold values from -1.75 to 1.75
- w_gate_up: bfloat16 [768, 2, 2048], P('col', None, 'row'), may hold values from -0.21875 to 0.21875
- w_down: bfloat16 [2048, 768], P('row', 'col'), may hold values from -0.125 to 0.125
- gain_attn: bfloat16 [768], P('row'), may hold values from 0.5 to 1.5
- gain_mlp: bfloat16 [768], P('row'), may hold values from 0.5 to 1.5
- cotangent: bfloat16 [32, 768, 1024], P(('dp', 'col'), 'row'), may hold values from -6 to 6
Outputs:
- block_out: bfloat16 [32, 768, 1024], P(('dp', 'col'), 'row')
- d_hidden_in: float32 [32, 768, 1024], P(('dp', 'col'), 'row')
- grad_qkv: float32 [768, 3, 768], P('col', None, 'row')
- grad_out: float32 [768, 768], P('row', 'col')
- grad_gate_up: float32 [768, 2, 2048], P('col', None, 'row')
- grad_down: float32 [2048, 768], P('row', 'col')
- grad_gain_attn: float32 [768], P('row')
- grad_gain_mlp: float32 [768], P('row')
The draws below stay inside these ranges and needn't reach their ends.
Inputs may be any that keep to these rules, and one draw needn't show every extreme that they name: `lengths`: each sequence's count of real tokens; slots from that count on are padding; some sequence is full and some holds exactly 256 tokens.
All inputs are finite; a program needn't handle non-finite values.
Results may differ from the reference program's by a relative error of at most 0.018.
Values may be sent and summed in bfloat16 or wider, within the bound.
A program may use at most 192 MiB of HBM per device.

```python
import math
import jax
import jax.numpy as jnp
from jax import lax

D = 768
HEADS = 12
HEAD_DIM = 64
FF = 2048
LEN = 1024
SEQS = 32


def draw_lengths(key, part):
    key = jax.random.fold_in(key, 7)
    first_key, second_key = jax.random.split(key)
    counts = jax.random.randint(first_key, (SEQS,), LEN // 4, LEN + 1)
    chosen = jax.random.permutation(second_key, SEQS)
    places = jnp.arange(SEQS)
    counts = jnp.where(places == chosen[0], LEN, counts)
    counts = jnp.where(places == chosen[1], LEN // 4, counts)
    return counts.astype(jnp.int32)


def levels(stream_key, extent, shards, low, largest):
    loudness, own = 1.0, jax.random.fold_in(stream_key, 6)
    for dim, blocks in shards:
        heights = jnp.exp(jax.random.uniform(jax.random.fold_in(own, dim), (blocks,), jnp.float32, low / len(shards), largest / len(shards)))
        loudness = loudness * jnp.repeat(heights, extent[dim] // blocks).reshape([-1 if axis == dim else 1 for axis in range(len(extent))])
    return loudness


def gaussian(key, extent, deviation, limit, cuts=(), kind=jnp.bfloat16):
    level = levels(key, extent, cuts, -0.22, 0.18) if cuts else 1.0
    array = jax.random.normal(key, extent, jnp.float32) * deviation * level
    return jnp.minimum(jnp.maximum(array, -limit), limit).astype(kind)


def setup_inputs(seed: int = 0) -> dict:
    splits = jax.random.split(jax.random.key(seed), 10)
    hidden_in = gaussian(splits[0], (SEQS, D, LEN), 1.0, 6.0, ((0, 8), (1, 4)))
    lengths = draw_lengths(jax.random.fold_in(splits[9], 71), 0)
    w_qkv = gaussian(splits[2], (D, 3, D), D ** -0.5, 0.21875, ((0, 4), (2, 4)))
    w_out = gaussian(splits[3], (D, D), (max(1, D * 16 // LEN)) ** -0.5, 1.75, ((0, 4), (1, 4)))
    w_gate_up = gaussian(splits[4], (D, 2, FF), D ** -0.5, 0.21875, ((0, 4), (2, 4)))
    w_down = gaussian(splits[5], (FF, D), FF ** -0.5, 0.125, ((0, 4), (1, 4)))
    gain_attn = jnp.clip(1.0 + 0.1 * jax.random.normal(splits[6], (D,), jnp.float32), 0.5, 1.5).astype(jnp.bfloat16)
    gain_mlp = jnp.clip(1.0 + 0.1 * jax.random.normal(splits[7], (D,), jnp.float32), 0.5, 1.5).astype(jnp.bfloat16)
    cotangent = gaussian(splits[8], (SEQS, D, LEN), 1.0, 6.0, ((0, 8), (1, 4)))
    return {"hidden_in": hidden_in, "lengths": lengths, "w_qkv": w_qkv, "w_out": w_out, "w_gate_up": w_gate_up, "w_down": w_down, "gain_attn": gain_attn, "gain_mlp": gain_mlp, "cotangent": cotangent}


EPS = 1e-05
HIGHEST = lax.Precision.HIGHEST

@jax.custom_vjp
def low(v):
    return lax.optimization_barrier(v.astype(jnp.bfloat16)).astype(jnp.float32)

@jax.custom_vjp
def low_back(v):
    return v

def low_keep(v):
    return (low(v), None)

def low_pass(kept, grad):
    return (grad,)

def back_keep(v):
    return (v, None)

def back_low(kept, grad):
    return (low(grad),)
low.defvjp(low_keep, low_pass)
low_back.defvjp(back_keep, back_low)

def rope_tables(length):
    half_dim = HEAD_DIM // 2
    frequency = jnp.exp(jnp.arange(half_dim, dtype=jnp.float32) * (-2.0 * math.log(10000.0) / HEAD_DIM))
    angles = jnp.arange(length, dtype=jnp.float32)[:, None] * frequency[None, :]
    return (jnp.cos(angles)[:, None, :], jnp.sin(angles)[:, None, :])

def rotate(values, cos_table, sin_table):
    half_dim = values.shape[-1] // 2
    first_half = values[..., :half_dim]
    second_half = values[..., half_dim:]
    return jnp.concatenate([first_half * cos_table - second_half * sin_table, second_half * cos_table + first_half * sin_table], axis=-1)

def rms(values, gain):
    return values * lax.rsqrt(lax.optimization_barrier(jnp.mean(values * values, axis=-1, keepdims=True)) + EPS) * gain

def visible(first_row, row_count, length, valid_len):
    query_pos = first_row + jnp.arange(row_count, dtype=jnp.int32)
    key_pos = jnp.arange(length, dtype=jnp.int32)
    return (key_pos[None, :] <= query_pos[:, None]) & (key_pos[None, :] < valid_len)

def attention(queries, key_rot, values, lengths):
    group_count = queries.shape[0]
    block_rows = min(512, LEN)
    blocks = LEN // block_rows
    scaling = 1.0 / math.sqrt(HEAD_DIM)
    flat_q = queries.reshape(group_count * blocks, block_rows, HEADS, HEAD_DIM)

    @jax.checkpoint
    def block_out(q_blk, k_seq, v_seq, valid_len, first_row):
        scores = low_back(jnp.einsum('qhe,khe->hqk', q_blk, k_seq, precision=HIGHEST) * scaling)
        allowed = visible(first_row, block_rows, LEN, valid_len)
        scores = jnp.where(allowed[None], scores, -1e+30)
        probs = low(jax.nn.softmax(scores, axis=-1))
        return jnp.einsum('hqk,khe->qhe', probs, v_seq, precision=HIGHEST)

    def per_block(position):
        seq_id = position // blocks
        return block_out(flat_q[position], key_rot[seq_id], values[seq_id], lengths[seq_id], position % blocks * block_rows)
    mixed_out = lax.map(per_block, jnp.arange(group_count * blocks, dtype=jnp.int32))
    return mixed_out.reshape(group_count, LEN, HEADS * HEAD_DIM)

def layer_forward(hidden, lengths, w_qkv, w_out, w_gate_up, w_down, gain_attn, gain_mlp):
    group_count = hidden.shape[0]
    cos_table, sin_table = rope_tables(LEN)
    dims_four = (group_count, LEN, HEADS, HEAD_DIM)
    normed_one = low(rms(hidden, gain_attn))
    projected = jnp.einsum('gld,dcf->glcf', normed_one, w_qkv, precision=HIGHEST)
    queries = low(rotate(low_back(projected[:, :, 0]).reshape(dims_four), cos_table, sin_table))
    key_rot = low(rotate(low_back(projected[:, :, 1]).reshape(dims_four), cos_table, sin_table))
    values = low(low_back(projected[:, :, 2])).reshape(dims_four)
    attended = low(low_back(attention(queries, key_rot, values, lengths)))
    middle = hidden + low_back(jnp.einsum('gld,de->gle', attended, w_out, precision=HIGHEST))
    normed_two = low(rms(middle, gain_mlp))
    gate_up = jnp.einsum('gld,dcf->glcf', normed_two, w_gate_up, precision=HIGHEST)
    gate_pre = low_back(gate_up[:, :, 0])
    up_pre = low_back(gate_up[:, :, 1])
    hidden_act = low(jax.nn.silu(gate_pre) * up_pre)
    return middle + low_back(jnp.einsum('glf,fd->gld', hidden_act, w_down, precision=HIGHEST))

def reference(hidden_in, lengths, w_qkv, w_out, w_gate_up, w_down, gain_attn, gain_mlp, cotangent):
    group_size = math.gcd(SEQS, max(1, 4096 // LEN))
    step_count = SEQS // group_size
    params = tuple((matrix.astype(jnp.float32) for matrix in (w_qkv, w_out, w_gate_up, w_down, gain_attn, gain_mlp)))
    inputs = hidden_in.astype(jnp.float32).transpose(0, 2, 1).reshape(step_count, group_size, LEN, D)
    incoming = cotangent.astype(jnp.float32).transpose(0, 2, 1).reshape(step_count, group_size, LEN, D)
    group_lens = lengths.reshape(step_count, group_size)

    def scan_step(carry, pieces):
        group_in, group_ct, group_len = pieces

        def forward(group_x, *weights_all):
            return layer_forward(group_x, group_len, *weights_all)
        result, pullback = jax.vjp(forward, group_in, *params)
        grads = pullback(group_ct)
        carry = tuple((running + fresh for running, fresh in zip(carry, grads[1:])))
        return (carry, (result, grads[0]))
    zeros = tuple((jnp.zeros(matrix.shape, jnp.float32) for matrix in params))
    totals, (results, d_inputs) = lax.scan(scan_step, zeros, (inputs, incoming, group_lens))
    block_out = results.reshape(SEQS, LEN, D).transpose(0, 2, 1).astype(jnp.bfloat16)
    d_hidden_in = d_inputs.reshape(SEQS, LEN, D).transpose(0, 2, 1)
    return (block_out, d_hidden_in, totals[0], totals[1], totals[2], totals[3], totals[4], totals[5])
```

```python
import math

import jax
import jax.numpy as jnp
from jax import lax
from jax.sharding import PartitionSpec as P

EPS = 1e-05
HEAD_DIM = 64
ALL = ("dp", "row", "col")
F32, BF16 = jnp.float32, jnp.bfloat16


def dot(a, b, contract):
    return lax.dot_general(a, b, ((contract[:1], contract[1:]), ((), ())), preferred_element_type=F32)


def rope_tables(length):
    half = HEAD_DIM // 2
    freq = jnp.exp(jnp.arange(half, dtype=F32) * (-2.0 * math.log(10000.0) / HEAD_DIM))
    angles = freq[:, None] * jnp.arange(length, dtype=F32)[None, :]
    return jnp.cos(angles), jnp.sin(angles)


def rope(v, cos, sin, sign):
    parts = v.reshape(-1, 2, HEAD_DIM // 2, v.shape[-1])
    a, b = parts[:, 0], parts[:, 1]
    out = jnp.stack([a * cos - sign * b * sin, b * cos + sign * a * sin], axis=1)
    return out.reshape(v.shape)


def norm(x, gain):
    r = lax.rsqrt(jnp.mean(x * x, axis=0, keepdims=True) + EPS)
    return r, (x * r * gain).astype(BF16)


def norm_back(d_normed, x, r, gain):
    unit = x * r
    d_unit = d_normed * gain
    inner = jnp.mean(d_unit * unit, axis=0, keepdims=True)
    return r * (d_unit - unit * inner), jnp.sum(d_normed * unit, axis=1)


def shards(hidden_in, lengths, w_qkv, w_out, w_gate_up, w_down, gain_attn, gain_mlp, cotangent):
    rows, cols = lax.axis_size("row"), lax.axis_size("col")
    depth, _, wide = w_qkv.shape
    ff = w_gate_up.shape[2]
    me = lax.axis_index("row")
    mine = jnp.concatenate(
        [w_out.T, w_qkv.reshape(depth, 3 * wide), w_gate_up.reshape(depth, 2 * ff), w_down.T], axis=1
    )
    half = depth // 2
    part = lax.dynamic_slice_in_dim(mine, lax.axis_index("dp") * half, half, 0)
    whole = lax.all_gather(part, ALL, axis=0)
    whole = whole.reshape(2, rows, cols, half, -1).transpose(1, 2, 0, 3, 4).reshape(rows, cols * depth, -1)
    gains = lax.all_gather(jnp.stack([gain_attn, gain_mlp]), "row", axis=1, tiled=True).astype(F32)
    gain_one, gain_two = gains[0][:, None], gains[1][:, None]
    x = lax.all_to_all(hidden_in, "row", split_axis=0, concat_axis=1, tiled=True)[0]
    g = lax.all_to_all(cotangent, "row", split_axis=0, concat_axis=1, tiled=True)[0]
    valid = lengths[me]
    length = x.shape[1]
    cos, sin = rope_tables(length)
    x = x.astype(F32)
    r_one, n_one = norm(x, gain_one)
    key_pos = jnp.arange(length)[:, None]
    seen = (key_pos <= key_pos.T) & (key_pos < valid)
    scale = 1.0 / math.sqrt(HEAD_DIM)
    kept, attn = [], []
    heads = wide // HEAD_DIM
    for r in range(rows):
        proj = dot(whole[r][:, wide : 4 * wide], n_one, (0, 0))
        q = rope(proj[:wide], cos, sin, 1.0).astype(BF16).reshape(heads, HEAD_DIM, length)
        k = rope(proj[wide : 2 * wide], cos, sin, 1.0).astype(BF16).reshape(heads, HEAD_DIM, length)
        v = proj[2 * wide :].astype(BF16).reshape(heads, HEAD_DIM, length)
        s = jnp.einsum("hek,heq->hkq", k, q, preferred_element_type=F32) * scale
        s = jnp.where(seen, s, -1e30)
        top = jnp.max(s, axis=1, keepdims=True)
        lse = top + jnp.log(jnp.sum(jnp.exp(s - top), axis=1, keepdims=True))
        p = jnp.exp(s - lse).astype(BF16)
        o = jnp.einsum("hek,hkq->heq", v, p, preferred_element_type=F32).astype(BF16)
        kept.append((q, k, v, lse))
        attn.append(o.reshape(wide, length))
    middle = x
    for r in range(rows):
        middle = middle + dot(whole[r][:, :wide], attn[r], (1, 0))
    r_two, n_two = norm(middle, gain_two)
    final, d_n_two, grads_m = middle, 0.0, []
    for r in range(rows):
        w_gu, w_dn = whole[r][:, 4 * wide : 4 * wide + 2 * ff], whole[r][:, 4 * wide + 2 * ff :]
        gu = dot(w_gu, n_two, (0, 0))
        gate, up = gu[:ff], gu[ff:]
        sig = jax.nn.sigmoid(gate)
        silu = gate * sig
        hid = (silu * up).astype(BF16)
        final = final + dot(w_dn, hid, (1, 0))
        d_hid = dot(w_dn, g, (0, 0))
        d_gu = jnp.concatenate([d_hid * up * sig * (1.0 + gate * (1.0 - sig)), d_hid * silu]).astype(BF16)
        d_n_two = d_n_two + dot(w_gu, d_gu, (1, 0))
        grads_m.append(jnp.concatenate([dot(n_two, d_gu, (1, 1)), dot(g, hid, (1, 1))], axis=1).astype(BF16))
    dv_two, grad_gain_two = norm_back(d_n_two, middle, r_two, gain_two)
    d_middle = g.astype(F32) + dv_two
    d_branch = d_middle.astype(BF16)
    d_n_one, grads = 0.0, []
    for r in range(rows):
        q, k, v, lse = kept[r]
        d_o = dot(whole[r][:, :wide], d_branch, (0, 0)).astype(BF16).reshape(heads, HEAD_DIM, length)
        s = jnp.einsum("hek,heq->hkq", k, q, preferred_element_type=F32) * scale
        p = jnp.exp(jnp.where(seen, s, -1e30) - lse)
        d_p = jnp.einsum("hek,heq->hkq", v, d_o, preferred_element_type=F32)
        inner = jnp.sum(d_p * p, axis=1, keepdims=True)
        d_s = (p * (d_p - inner)).astype(BF16)
        d_q = jnp.einsum("hek,hkq->heq", k, d_s, preferred_element_type=F32) * scale
        d_k = jnp.einsum("heq,hkq->hek", q, d_s, preferred_element_type=F32) * scale
        d_v = jnp.einsum("heq,hkq->hek", d_o, p.astype(BF16), preferred_element_type=F32)
        d_proj = jnp.concatenate(
            [
                rope(d_q.reshape(wide, length), cos, sin, -1.0),
                rope(d_k.reshape(wide, length), cos, sin, -1.0),
                d_v.reshape(wide, length),
            ]
        ).astype(BF16)
        d_n_one = d_n_one + dot(whole[r][:, wide : 4 * wide], d_proj, (1, 0))
        grads.append(
            jnp.concatenate(
                [dot(d_branch, attn[r], (1, 1)).astype(BF16), dot(n_one, d_proj, (1, 1)).astype(BF16), grads_m[r]], axis=1
            )
        )
    dv_one, grad_gain_one = norm_back(d_n_one, x, r_one, gain_one)
    d_x = (d_middle + dv_one).astype(BF16)
    out = lax.all_to_all(final.astype(BF16)[None], "row", split_axis=1, concat_axis=0, tiled=True)
    d_x = lax.all_to_all(d_x[None], "row", split_axis=1, concat_axis=0, tiled=True).astype(F32)
    grad = jnp.stack(grads).reshape(rows, cols, 2, half, -1).transpose(2, 0, 1, 3, 4)
    grad = lax.psum_scatter(grad.reshape(2 * rows * cols * half, -1), ALL, scatter_dimension=0, tiled=True)
    grad = lax.all_gather(grad, "dp", axis=0, tiled=True).astype(F32)
    gain_grads = lax.psum(jnp.stack([grad_gain_one, grad_gain_two]), ALL)
    gain_grads = lax.dynamic_slice_in_dim(gain_grads, me * wide, wide, 1)
    return (
        out,
        d_x,
        grad[:, wide : 4 * wide].reshape(depth, 3, wide),
        grad[:, :wide].T,
        grad[:, 4 * wide : 4 * wide + 2 * ff].reshape(depth, 2, ff),
        grad[:, 4 * wide + 2 * ff :].T,
        gain_grads[0],
        gain_grads[1],
    )


def solution(mesh):
    tokens, wide = P(("dp", "col"), "row", None), P("col", None, "row")
    back, gain = P("row", "col"), P("row")
    return jax.shard_map(
        shards,
        mesh=mesh,
        in_specs=(tokens, P(("dp", "col")), wide, back, wide, back, gain, gain, tokens),
        out_specs=(tokens, tokens, wide, back, wide, back, gain, gain),
        check_vma=False,
    )
```

```python
import functools
import math

import jax
import jax.numpy as jnp
from jax import lax
from jax.experimental import pallas as pl
from jax.experimental.pallas import tpu as pltpu
from jax.sharding import PartitionSpec as P

EPS = 1e-05
E = 64
C = 256
LOG2E = math.log2(math.e)
F32, BF16 = jnp.float32, jnp.bfloat16
N_COPIES = 128


def dg(a, b, contract):
    return lax.dot_general(a, b, ((contract[:1], contract[1:]), ((), ())), preferred_element_type=F32)


def rope(v, cos, sin, sign):
    half = v.shape[0] // 2
    a, b = v[:half], v[half:]
    return jnp.concatenate([a * cos - sign * (b * sin), b * cos + sign * (a * sin)], axis=0)


def pack_rows(values, width):
    row = lax.broadcasted_iota(jnp.int32, (16, width), 0)
    out = jnp.zeros((16, width), F32)
    for i, v in enumerate(values):
        out = jnp.where(row == i, v, out)
    return out.astype(BF16)


def split3(v):
    hi = v.astype(BF16).astype(F32)
    mid = (v - hi).astype(BF16).astype(F32)
    return hi, mid, v - hi - mid


def layer(groups, refs):
    s = refs
    d, length = s.N1.shape
    wide = s.X.shape[1]
    heads = wide // E
    ff = s.HD.shape[0] // 3
    la = 4 * wide
    n_blk = length // C

    h, r, c = lax.axis_index("dp"), lax.axis_index("row"), lax.axis_index("col")
    cc, ci = c // groups, c % groups
    col = {1: cc + 1 - 2 * (cc % 2), 2: (cc + 2) % 4, 3: 3 - cc}
    row = {1: r + 1 - 2 * (r % 2), 2: (r + 2) % 4, 3: 3 - r}
    a, b = 1 + h, 2 - h
    to = {
        "dp": {"dp": 1 - h},
        "z1": {"col": col[1] * groups + ci},
        "z2": {"col": col[2] * groups + ci},
        "r1": {"row": row[1]},
        "r2": {"row": row[2]},
        "r3": {"row": row[3]},
        "a": {"row": (1 - h) * row[1] + h * row[2]},
        "b": {"row": (1 - h) * row[2] + h * row[1]},
    }
    copies = {}

    def send(name, src, dst, where):
        assert name not in copies, name
        n = len(copies)
        copies[name] = pltpu.make_async_remote_copy(
            src_ref=src,
            dst_ref=dst,
            send_sem=s.ssem.at[n],
            recv_sem=s.rsem.at[n],
            device_id=to[where],
            device_id_type=pl.DeviceIdType.MESH,
        )
        copies[name].start()

    def local(name, src, dst):
        assert name not in copies, name
        n = len(copies)
        copies[name] = pltpu.make_async_copy(src, dst, s.ssem.at[n])
        copies[name].start()

    def got(*names):
        for name in names:
            copies[name].wait_recv()

    def sent(*names):
        for name in names:
            copies[name].wait_send()

    def done(*names):
        for name in names:
            copies[name].wait()

    def add(dst, src):
        dst[...] = (dst[...].astype(F32) + src[...].astype(F32)).astype(BF16)

    def phase(body):
        def run(*args):
            pl.when(r < 4)(functools.partial(body, *args))

        return run

    def w_a(i, lo=0, hi=la):
        return s.WA[i, :, :, :, lo:hi].reshape(d, hi - lo)

    def w_m(i, lo=0, hi=3 * ff):
        return s.WM[i, :, :, :, lo:hi].reshape(d, hi - lo)

    def put(ref, i, lo, value):
        n = value.shape[1]
        ref[i, :, :, :, lo : lo + n] = value.astype(BF16).reshape(4, 2, d // 8, n)

    def blocks():
        return [slice(j * C, (j + 1) * C) for j in range(n_blk)]

    def gain(which):
        return s.GAIN[...].reshape(d, s.GAIN.shape[-1])[:, which : which + 1].astype(F32)

    def x_of(sl):
        return s.X[:, :, sl].reshape(d, sl.stop - sl.start).astype(F32)

    @phase
    def setup():
        s.ATT[:, wide:] = jnp.zeros((4, s.ATT.shape[1] - wide, length), BF16)
        s.GG[0] = jnp.zeros((8, d), F32)
        pos = lax.broadcasted_iota(jnp.int32, (1, length), 1)
        bias = jnp.where(pos < s.lengths[r], 0.0, -1e30)
        shape = (4 * heads, 16, length)
        s.K[:, E:] = jnp.broadcast_to(pack_rows([bias, 1.0, 1.0, 1.0], length), shape)
        s.Q[:, E:] = jnp.broadcast_to(pack_rows([1.0], length), shape)
        s.V[:, E:] = jnp.broadcast_to(pack_rows([1.0, 1.0, 1.0], length), shape)

    @phase
    def norm(which):
        for sl in blocks():
            x = s.MID[:, sl] if which else x_of(sl)
            inv = lax.rsqrt(jnp.sum(x * x, axis=0, keepdims=True) * (1.0 / d) + EPS)
            s.R[which : which + 1, sl] = inv
            (s.N2 if which else s.N1)[:, sl] = (x * inv * gain(which)).astype(BF16)

    def halves():
        return [slice(0, length // 2), slice(length // 2, length)]

    @phase
    def project(i):
        for sl in halves():
            p = dg(w_a(i), s.N1[:, sl], (0, 0))
            cos, sin = s.cos[:, sl], s.sin[:, sl]
            for k in range(heads):
                part = [p[n * wide + k * E : n * wide + (k + 1) * E] for n in (1, 2, 3)]
                s.Q[heads * i + k, :E, sl] = (rope(part[0], cos, sin, 1.0) * (LOG2E / math.sqrt(E))).astype(BF16)
                s.K[heads * i + k, :E, sl] = rope(part[1], cos, sin, 1.0).astype(BF16)
                s.V[heads * i + k, :E, sl] = part[2].astype(BF16)

    def causal():
        return lax.broadcasted_iota(jnp.int32, (C, C), 0) <= lax.broadcasted_iota(jnp.int32, (C, C), 1)

    @phase
    def attend(i):
        tri = causal()
        items = [(k, j) for k in range(heads) for j in range(n_blk)]
        lse = []

        def scores(k, j):
            return dg(s.K[heads * i + k, :, : (j + 1) * C], s.Q[heads * i + k, :, j * C : (j + 1) * C], (0, 0))

        def soft(v, j):
            n = j * C
            diag = jnp.where(tri, v[n:], -1e30)
            top = jnp.max(diag, axis=0, keepdims=True)
            if j:
                top = jnp.maximum(top, jnp.max(v[:n], axis=0, keepdims=True))
            e = jnp.exp2(diag - top).astype(BF16)
            if j:
                e = jnp.concatenate([jnp.exp2(v[:n] - top).astype(BF16), e], axis=0)
            return top, e

        def mix(k, j, top, e):
            sl = slice(j * C, (j + 1) * C)
            o = dg(s.V[heads * i + k, :, : (j + 1) * C], e, (1, 0))
            total = o[E : E + 1]
            s.ATT[i, k * E : (k + 1) * E, sl] = (o[:E] * (1.0 / total)).astype(BF16)
            lse.append((k, sl, pack_rows([1.0, *split3(-(top + jnp.log2(total)))], C)))

        held, now = None, scores(*items[0])
        for n, (k, j) in enumerate(items):
            later = scores(*items[n + 1]) if n + 1 < len(items) else None
            top, e = soft(now, j)
            if held:
                mix(*held)
            held, now = (k, j, top, e), later
        mix(*held)
        for k, sl, rows in lse:
            s.Q[heads * i + k, E:, sl] = rows

    @phase
    def out_project():
        for i in range(4):
            for sl in halves():
                y = dg(w_a(i, 0, s.ATT.shape[1]), s.ATT[i, :, sl], (1, 0))
                s.MID[:, sl] = (s.MID[:, sl] if i else s.X[:, :, sl].reshape(d, length // 2).astype(F32)) + y

    @phase
    def mlp(i):
        first = i == 0

        def dots(sl):
            gu = dg(w_m(i, 0, 2 * ff), s.N2[:, sl], (0, 0))
            return gu, dg(w_m(i, 2 * ff), s.G[:, :, sl].reshape(d, C), (0, 0))

        def mix(sl, gu, d_hid):
            gate, up = gu[:ff], gu[ff:]
            sig = 1.0 / (1.0 + jnp.exp(-gate))
            silu = gate * sig
            s.HD[:ff, sl] = (silu * up).astype(BF16)
            s.HD[ff : 2 * ff, sl] = (d_hid * up * (sig + silu * (1.0 - sig))).astype(BF16)
            s.HD[2 * ff :, sl] = (d_hid * silu).astype(BF16)

        now = dots(blocks()[0])
        for j, sl in enumerate(blocks()):
            later = dots(blocks()[j + 1]) if j + 1 < n_blk else None
            mix(sl, *now)
            now = later
        for sl in halves():
            y = dg(w_m(i, 2 * ff), s.HD[:ff, sl], (1, 0))
            s.FIN[:, sl] = (s.MID if first else s.FIN)[:, sl] + y
            z = dg(w_m(i, 0, 2 * ff), s.HD[ff:, sl], (1, 0))
            s.DN[:, sl] = z if first else s.DN[:, sl] + z

    @phase
    def mlp_grad(i):
        put(s.WM, i, 0, dg(s.N2[...], s.HD[ff : 2 * ff], (1, 1)))
        put(s.WM, i, ff, dg(s.N2[...], s.HD[2 * ff :], (1, 1)))
        put(s.WM, i, 2 * ff, dg(s.G[...].reshape(d, length), s.HD[:ff], (1, 1)))

    @phase
    def norm_back(which):
        total = jnp.zeros((d, 128), F32)
        for j in range(0, length, 128):
            sl = slice(j, j + 128)
            dn = (s.DN if which else s.FIN)[:, sl]
            inv = s.R[which : which + 1, sl]
            unit = (s.MID[:, sl] if which else x_of(sl)) * inv
            e = dn * gain(which)
            inner = jnp.sum(e * unit, axis=0, keepdims=True) * (1.0 / d)
            dv = inv * (e - unit * inner)
            total = total + dn * unit
            if which:
                dm = s.G[:, :, sl].reshape(d, 128).astype(F32) + dv
                s.DN[:, sl] = dm
                s.N2[:, sl] = dm.astype(BF16)
            else:
                s.HD[d:, sl] = (s.DN[:, sl] + dv).astype(BF16)
        s.GG[0, which : which + 1, :] = jnp.sum(total.T, axis=0, keepdims=True)

    @phase
    def attend_back(i, first):
        tri, dr = causal(), E + 16
        d_o = dg(w_a(i, 0, s.ATT.shape[1]), s.N2[...], (0, 0))[:wide].astype(BF16)
        for k in range(heads):
            part = d_o[k * E : (k + 1) * E]
            s.HD[d + k * dr : d + k * dr + E] = part
            inner = jnp.sum(part.astype(F32) * s.ATT[i, k * E : (k + 1) * E].astype(F32), axis=0, keepdims=True)
            s.HD[d + k * dr + E : d + (k + 1) * dr] = pack_rows(split3(-inner), length)
        items = [(k, j) for k in range(heads) for j in range(n_blk)]

        def start(k, j):
            n, sl, g = (j + 1) * C, slice(j * C, (j + 1) * C), heads * i + k
            return dg(s.K[g, :, :n], s.Q[g, :, sl], (0, 0)), dg(s.V[g, :, :n], s.HD[d + k * dr : d + (k + 1) * dr, sl], (0, 0))

        def finish(k, j, sc, dp):
            n, sl, g = (j + 1) * C, slice(j * C, (j + 1) * C), heads * i + k
            p = jnp.where(tri, jnp.exp2(sc[n - C :]), 0.0)
            if j:
                p = jnp.concatenate([jnp.exp2(sc[: n - C]), p], axis=0)
            ds, p = (p * dp).astype(BF16), p.astype(BF16)
            s.MID[k * E : (k + 1) * E, sl] = dg(s.K[g, :E, :n], ds, (1, 0))
            dk, dv = dg(s.Q[g, :E, sl], ds, (1, 1)), dg(s.HD[d + k * dr : d + k * dr + E, sl], p, (1, 1))
            at = slice(wide + k * E, wide + (k + 1) * E), slice(2 * wide + k * E, 2 * wide + (k + 1) * E)
            if j == 0:
                s.MID[at[0]] = jnp.zeros((E, length), F32)
                s.MID[at[1]] = jnp.zeros((E, length), F32)
            s.MID[at[0], :n] += dk
            s.MID[at[1], :n] += dv

        now = start(*items[0])
        for n, (k, j) in enumerate(items):
            later = start(*items[n + 1]) if n + 1 < len(items) else None
            finish(k, j, *now)
            now = later
        for sl in halves():
            cos, sin = s.cos[:, sl], s.sin[:, sl]
            dp = [jnp.zeros((wide, length // 2), BF16)]
            for n, scale in enumerate((1.0 / math.sqrt(E), 1.0 / LOG2E, None)):
                for k in range(heads):
                    v = s.MID[n * wide + k * E : n * wide + (k + 1) * E, sl]
                    dp.append((v if scale is None else rope(v * scale, cos, sin, -1.0)).astype(BF16))
            dp = jnp.concatenate(dp, axis=0)
            s.RDM[:2, :, :, sl] = dp.reshape(2, 4, d // 8, length // 2)
            z = dg(w_a(i), dp, (1, 0))
            s.FIN[:, sl] = z if first else s.FIN[:, sl] + z
        dp = s.RDM[:2, :, :, :length].reshape(d, length)
        gq, go = dg(s.N1[...], dp, (1, 1)), dg(s.N2[...], s.ATT[i], (1, 1))
        n = go.shape[1]
        put(s.WA, i, 0, gq[:, :n] + go)
        put(s.WA, i, n, gq[:, n:])

    def own(ref, lo, hi):
        return ref.at[h, :, lo:hi]

    def spread(name, src, dst):
        for k in (1, 2, 3):
            send(f"{name}{k}", src(row[k]), dst(r), f"r{k}")
        local(f"{name}0", src(r), dst(r))

    def spread_got(name):
        got(*(f"{name}{k}" for k in (1, 2, 3)))
        done(f"{name}0")

    def spread_sent(name):
        sent(*(f"{name}{k}" for k in (1, 2, 3)))

    def fold(tag, ref, recv, i):
        got(f"{tag}_fold{i}")
        add(ref.at[i, :, h], recv.at[i])

    def fold_send(tag, ref, recv, i):
        send(f"{tag}_fold{i}", ref.at[i, :, 1 - h], recv.at[i], "dp")

    def b_send(tag, ref, recv, slot, k):
        send(f"{tag}_half{k}", ref.at[slot, :, h], recv.at[k], "b")

    def z1_send(tag, ref, recv, slot, k):
        send(f"{tag}_far{k}", ref.at[slot, col[3], h], recv.at[k, 1], "z1")
        send(f"{tag}_near{k}", ref.at[slot, col[1], h], recv.at[k, 0], "z1")

    def z2_send(tag, ref, recv1, recv, slot, k):
        got(f"{tag}_far{k}")
        add(ref.at[slot, col[2], h], recv1.at[k, 1])
        send(f"{tag}_last{k}", ref.at[slot, col[2], h], recv.at[k], "z2")

    def z_finish(tag, ref, recv1, recv2, slot, k):
        got(f"{tag}_near{k}", f"{tag}_last{k}")
        ref[slot, cc, h] = (
            ref[slot, cc, h].astype(F32) + recv1[k, 0].astype(F32) + recv2[k].astype(F32)
        ).astype(BF16)

    def b_fold(tag, ref, recv, slot, k):
        got(f"{tag}_half{k}")
        add(ref.at[slot, :, h], recv.at[k])

    barrier = pltpu.get_barrier_semaphore()
    friends = ("dp", "z1", "z2", "r1", "r2", "r3")
    for name in friends:
        pl.semaphore_signal(barrier, inc=1, device_id=to[name], device_id_type=pl.DeviceIdType.MESH)
    pl.semaphore_wait(barrier, len(friends))

    spread("hid", lambda i: s.hidden.at[i], lambda i: s.X.at[i])
    spread("gain", lambda i: s.gains, lambda i: s.GAIN.at[i])
    send("Az2", own(s.w, 0, la), s.WA.at[0, cc, h], "z2")
    send("Az1", own(s.w, 0, la), s.WA.at[0, cc, h], "z1")
    local("A0", own(s.w, 0, la), s.WA.at[0, cc, h])
    send("Ma", own(s.w, la, la + 3 * ff), s.WM.at[a, cc, h], "a")
    local("M0", own(s.w, la, la + 3 * ff), s.WM.at[0, cc, h])
    setup()
    got("Az2")
    send("Az12", s.WA.at[0, col[2], h], s.WA.at[0, col[2], h], "z1")
    done("M0")
    send("Mz2_0", s.WM.at[0, cc, h], s.WM.at[0, cc, h], "z2")
    got("Az1", "Az12")
    done("A0")
    send("Ad0", s.WA.at[0, :, h], s.WA.at[0, :, h], "dp")
    send("Mz1_0", s.WM.at[0, cc, h], s.WM.at[0, cc, h], "z1")
    got("Ma")
    send("Mz2_a", s.WM.at[a, cc, h], s.WM.at[a, cc, h], "z2")
    send("Mz1_a", s.WM.at[a, cc, h], s.WM.at[a, cc, h], "z1")
    spread_got("hid")
    spread_got("gain")
    send("Aa", s.WA.at[0, :, h], s.WA.at[a, :, h], "a")
    send("Ab0", s.WA.at[0, :, h], s.WA.at[b, :, h], "b")
    norm(0)
    got("Ad0")
    project(0)
    attend(0)
    got("Aa")
    send("Ada", s.WA.at[a, :, h], s.WA.at[a, :, h], "dp")
    send("Aba", s.WA.at[a, :, h], s.WA.at[3, :, h], "b")
    got("Ab0")
    send("Adb", s.WA.at[b, :, h], s.WA.at[b, :, h], "dp")
    spread("cot", lambda i: s.cot.at[i], lambda i: s.G.at[i])
    got("Mz2_0")
    send("Mz12_0", s.WM.at[0, col[2], h], s.WM.at[0, col[2], h], "z1")
    got("Ada", "Adb")
    project(1)
    attend(1)
    got("Mz2_a")
    send("Mz12_a", s.WM.at[a, col[2], h], s.WM.at[a, col[2], h], "z1")
    project(2)
    attend(2)
    got("Aba")
    send("Ad3", s.WA.at[3, :, h], s.WA.at[3, :, h], "dp")
    got("Ad3")
    project(3)
    attend(3)
    got("Mz1_0", "Mz12_0")
    send("Md0", s.WM.at[0, :, h], s.WM.at[0, :, h], "dp")
    send("Mb0", s.WM.at[0, :, h], s.WM.at[b, :, h], "b")
    out_project()
    norm(1)
    got("Mz1_a", "Mz12_a")
    send("Mda", s.WM.at[a, :, h], s.WM.at[a, :, h], "dp")
    send("Mba", s.WM.at[a, :, h], s.WM.at[3, :, h], "b")
    got("Md0")
    spread_got("cot")
    mlp(0)
    got("Mb0")
    send("Mdb", s.WM.at[b, :, h], s.WM.at[b, :, h], "dp")
    sent("Mz2_0", "Mz1_0", "Mz12_0", "Md0", "Mb0")
    mlp_grad(0)
    fold_send("M", s.WM, s.RDM, 0)
    got("Mda", "Mdb")
    mlp(1)
    sent("Mz2_a", "Mz1_a", "Mz12_a", "Mda", "Mdb", "Mba")
    mlp_grad(1)
    fold_send("M", s.WM, s.RDM, 1)
    fold("M", s.WM, s.RDM, 0)
    mlp(2)
    mlp_grad(2)
    fold_send("M", s.WM, s.RDM, 2)
    fold("M", s.WM, s.RDM, 1)
    got("Mba")
    send("Md3", s.WM.at[3, :, h], s.WM.at[3, :, h], "dp")
    got("Md3")
    mlp(3)
    fold("M", s.WM, s.RDM, 2)
    b_send("M", s.WM, s.RBM, b, 0)
    sent("Md3")
    mlp_grad(3)
    fold_send("M", s.WM, s.RDM, 3)
    spread_sent("cot")
    s.HD[:d] = s.FIN[...].astype(BF16)
    norm_back(1)
    fold("M", s.WM, s.RDM, 3)
    b_send("M", s.WM, s.RBM, 3, 1)
    for k in (1, 2, 3):
        send(f"out{k}", s.HD.at[pl.ds(pl.multiple_of(row[k] * wide, wide), wide)], s.out.at[r], f"r{k}")
    local("out0", s.HD.at[pl.ds(pl.multiple_of(r * wide, wide), wide)], s.out.at[r])
    sent("Az2", "Az1", "Az12", "Ad0", "Aa", "Ab0", "Ada", "Adb", "Aba", "Ad3")
    attend_back(3, True)
    fold_send("A", s.WA, s.RDA, 3)
    b_fold("M", s.WM, s.RBM, 0, 0)
    z1_send("M", s.WM, s.RZM, 0, 0)
    attend_back(1, False)
    fold_send("A", s.WA, s.RDA, 1)
    fold("A", s.WA, s.RDA, 3)
    b_send("A", s.WA, s.RBA, 3, 1)
    z2_send("M", s.WM, s.RZM, s.RYM, 0, 0)
    b_fold("M", s.WM, s.RBM, a, 1)
    z1_send("M", s.WM, s.RZM, a, 1)
    attend_back(2, False)
    fold_send("A", s.WA, s.RDA, 2)
    fold("A", s.WA, s.RDA, 1)
    fold("A", s.WA, s.RDA, 2)
    b_send("A", s.WA, s.RBA, b, 0)
    z2_send("M", s.WM, s.RZM, s.RYM, a, 1)
    b_fold("A", s.WA, s.RBA, a, 1)
    z1_send("A", s.WA, s.RZA, a, 1)
    attend_back(0, False)
    fold_send("A", s.WA, s.RDA, 0)
    norm_back(0)
    for k in (1, 2, 3):
        send(f"dx{k}", s.HD.at[pl.ds(pl.multiple_of(d + row[k] * wide, wide), wide)], s.dx.at[r], f"r{k}")
    local("dx0", s.HD.at[pl.ds(pl.multiple_of(d + r * wide, wide), wide)], s.dx.at[r])
    fold("A", s.WA, s.RDA, 0)
    b_fold("A", s.WA, s.RBA, 0, 0)
    z1_send("A", s.WA, s.RZA, 0, 0)
    z2_send("A", s.WA, s.RZA, s.RYA, a, 1)
    z_finish("M", s.WM, s.RZM, s.RYM, a, 1)
    send("Me", s.WM.at[a, cc, h], s.REM, "a")
    z_finish("M", s.WM, s.RZM, s.RYM, 0, 0)
    for n, name in enumerate(("dp", "r1", "r2", "z1", "z2")):
        send(f"gg{n}", s.GG.at[n], s.RG.at[n], name)
        got(f"gg{n}")
        s.GG[n + 1] = s.GG[n] + s.RG[n]
    z2_send("A", s.WA, s.RZA, s.RYA, 0, 0)
    z_finish("A", s.WA, s.RZA, s.RYA, a, 1)
    send("Ae", s.WA.at[a, cc, h], s.REA, "a")
    got("Me")
    add(s.WM.at[0, cc, h], s.REM)
    send("Mf", s.WM.at[0, cc, h], s.grads.at[h, :, la:], "dp")
    local("Mf0", s.WM.at[0, cc, h], s.grads.at[h, :, la:])
    z_finish("A", s.WA, s.RZA, s.RYA, 0, 0)
    got("Ae")
    add(s.WA.at[0, cc, h], s.REA)
    send("Af", s.WA.at[0, cc, h], s.grads.at[h, :, :la], "dp")
    local("Af0", s.WA.at[0, cc, h], s.grads.at[h, :, :la])
    local("gg", s.GG.at[5], s.gain_grads)
    done("gg", "Mf0", "Af0", "out0", "dx0")
    got("Mf", "Af")
    for name in ("out", "dx"):
        got(*(f"{name}{k}" for k in (1, 2, 3)))
        spread_sent(name)
    spread_sent("hid")
    spread_sent("gain")
    sent("Ma", "Me", "Mf", "Ae", "Af", *(f"gg{n}" for n in range(5)))
    for tag in "MA":
        sent(*(f"{tag}_fold{i}" for i in range(4)))
        sent(*(f"{tag}_{kind}{k}" for kind in ("half", "far", "near", "last") for k in (0, 1)))


class Refs:
    def __init__(self, names, refs):
        self.__dict__.update(zip(names, refs, strict=True))


INPUTS = ("lengths", "hidden", "cot", "w", "gains", "cos", "sin")
OUTPUTS = ("out", "dx", "grads", "gain_grads")


def shards(groups, hidden, lengths, w_qkv, w_out, w_gate_up, w_down, gain_attn, gain_mlp, cotangent):
    _, wide, length = hidden.shape
    d, ff = 4 * wide, w_gate_up.shape[2]
    rows = w_qkv.shape[0]
    w = jnp.concatenate(
        [w_out.T, w_qkv.reshape(rows, 3 * wide), w_gate_up.reshape(rows, 2 * ff), w_down.T], axis=1
    )
    cols = lax.axis_size("col")
    clubs = [[g * groups + i for i in range(groups)] for g in range(cols // groups)]
    if groups > 1:
        w = lax.all_gather(w, "col", axis_index_groups=clubs, axis=0, tiled=True)
    la, lm, eighth = 4 * wide, 3 * ff, d // 8
    gains = jnp.pad(jnp.stack([gain_attn, gain_mlp], axis=1), ((0, 0), (0, 126)))
    freq = jnp.exp(jnp.arange(E // 2, dtype=F32) * (-2.0 * math.log(10000.0) / E))
    angles = freq[:, None] * jnp.arange(length, dtype=F32)[None, :]
    heads = d // E
    scratch = {
        "WA": pltpu.VMEM((4, 4, 2, eighth, la), BF16),
        "WM": pltpu.VMEM((4, 4, 2, eighth, lm), BF16),
        "X": pltpu.VMEM((4, wide, length), BF16),
        "G": pltpu.VMEM((4, wide, length), BF16),
        "GAIN": pltpu.VMEM((4, wide, 128), BF16),
        "N1": pltpu.VMEM((d, length), BF16),
        "N2": pltpu.VMEM((d, length), BF16),
        "Q": pltpu.VMEM((heads, E + 16, length), BF16),
        "K": pltpu.VMEM((heads, E + 16, length), BF16),
        "V": pltpu.VMEM((heads, E + 16, length), BF16),
        "ATT": pltpu.VMEM((4, 256, length), BF16),
        "MID": pltpu.VMEM((d, length), F32),
        "FIN": pltpu.VMEM((d, length), F32),
        "DN": pltpu.VMEM((d, length), F32),
        "HD": pltpu.VMEM((3 * ff, length), BF16),
        "R": pltpu.VMEM((8, length), F32),
        "GG": pltpu.VMEM((6, 8, d), F32),
        "RG": pltpu.VMEM((5, 8, d), F32),
        "RDA": pltpu.VMEM((4, 4, eighth, la), BF16),
        "RDM": pltpu.VMEM((4, 4, eighth, lm), BF16),
        "RBA": pltpu.VMEM((2, 4, eighth, la), BF16),
        "RBM": pltpu.VMEM((2, 4, eighth, lm), BF16),
        "RZA": pltpu.VMEM((2, 2, eighth, la), BF16),
        "RZM": pltpu.VMEM((2, 2, eighth, lm), BF16),
        "RYA": pltpu.VMEM((2, eighth, la), BF16),
        "RYM": pltpu.VMEM((2, eighth, lm), BF16),
        "REA": pltpu.VMEM((eighth, la), BF16),
        "REM": pltpu.VMEM((eighth, lm), BF16),
        "ssem": pltpu.SemaphoreType.DMA((N_COPIES,)),
        "rsem": pltpu.SemaphoreType.DMA((N_COPIES,)),
    }

    def kernel(*refs):
        layer(groups, Refs((*INPUTS, *OUTPUTS, *scratch), refs))

    anywhere, vmem = pl.BlockSpec(memory_space=pl.ANY), pl.BlockSpec(memory_space=pltpu.VMEM)
    out, dx, grad, gain_grads = pl.pallas_call(
        kernel,
        out_shape=(
            jax.ShapeDtypeStruct(hidden.shape, BF16),
            jax.ShapeDtypeStruct(hidden.shape, BF16),
            jax.ShapeDtypeStruct((2, eighth, la + lm), BF16),
            jax.ShapeDtypeStruct((8, d), F32),
        ),
        in_specs=[pl.BlockSpec(memory_space=pltpu.SMEM), *[anywhere] * 4, vmem, vmem],
        out_specs=(anywhere,) * 4,
        scratch_shapes=list(scratch.values()),
        compiler_params=pltpu.CompilerParams(
            collective_id=0, has_side_effects=True, vmem_limit_bytes=63 * 2**20
        ),
    )(lengths, hidden, cotangent, w.reshape(2, eighth, la + lm), gains, jnp.cos(angles), jnp.sin(angles))
    grad = grad.reshape(d // 4, la + lm)
    gain_grads = lax.dynamic_slice_in_dim(gain_grads[:2], lax.axis_index("row") * wide, wide, 1)
    if groups > 1:
        grad = lax.psum_scatter(grad, "col", axis_index_groups=clubs, scatter_dimension=0, tiled=True)
        gain_grads = lax.psum(gain_grads, "col", axis_index_groups=clubs)
    grad = grad.astype(F32)
    return (
        out,
        dx.astype(F32),
        grad[:, wide:la].reshape(rows, 3, wide),
        grad[:, :wide].T,
        grad[:, la : la + 2 * ff].reshape(rows, 2, ff),
        grad[:, la + 2 * ff :].T,
        gain_grads[0],
        gain_grads[1],
    )


def solution(mesh):
    tokens, wide = P(("dp", "col"), "row", None), P("col", None, "row")
    back, gain = P("row", "col"), P("row")
    return jax.shard_map(
        functools.partial(shards, mesh.shape["col"] // 4),
        mesh=mesh,
        in_specs=(tokens, P(("dp", "col")), wide, back, wide, back, gain, gain, tokens),
        out_specs=(tokens, tokens, wide, back, wide, back, gain, gain),
        check_vma=False,
    )
```

```python
import functools
import math

import jax
import jax.numpy as jnp
import numpy as np
from jax import lax
from jax.experimental import pallas as pl
from jax.experimental.pallas import tpu as pltpu
from jax.sharding import PartitionSpec as P

EPS = 1e-05
E = 64
C = 256
LOG2E = math.log2(math.e)
F32, BF16 = jnp.float32, jnp.bfloat16
N_COPIES = 128


def dg(a, b, contract):
    return lax.dot_general(a, b, ((contract[:1], contract[1:]), ((), ())), preferred_element_type=F32)


def rope(v, cos, sin, sign):
    half = v.shape[0] // 2
    a, b = v[:half], v[half:]
    return jnp.concatenate([a * cos - sign * (b * sin), b * cos + sign * (a * sin)], axis=0)


def pack_rows(values, width):
    row = lax.broadcasted_iota(jnp.int32, (16, width), 0)
    out = jnp.zeros((16, width), F32)
    for i, v in enumerate(values):
        out = jnp.where(row == i, v, out)
    return out.astype(BF16)


def split3(v):
    hi = v.astype(BF16).astype(F32)
    mid = (v - hi).astype(BF16).astype(F32)
    return hi, mid, v - hi - mid


def layer(groups, refs):
    s = refs
    d, length = s.N1.shape
    wide = s.X.shape[1]
    heads = wide // E
    ff = s.HD.shape[0] // 3
    la, lm = 4 * wide, 3 * ff
    n_blk = length // C

    h, r, c = lax.axis_index("dp"), lax.axis_index("row"), lax.axis_index("col")
    cc, ci = c // groups, c % groups
    col = {1: cc + 1 - 2 * (cc % 2), 2: (cc + 2) % 4, 3: 3 - cc}
    row = {1: r + 1 - 2 * (r % 2), 2: (r + 2) % 4, 3: 3 - r}
    a, b = 1 + h, 2 - h
    to = {
        "dp": {"dp": 1 - h},
        "z1": {"col": col[1] * groups + ci},
        "z2": {"col": col[2] * groups + ci},
        "r1": {"row": row[1]},
        "r2": {"row": row[2]},
        "r3": {"row": row[3]},
        "a": {"row": (1 - h) * row[1] + h * row[2]},
        "b": {"row": (1 - h) * row[2] + h * row[1]},
    }
    copies = {}
    parts = {"A": (0, la), "M": (la, la + lm)}

    def send(name, src, dst, where):
        assert name not in copies, name
        n = len(copies)
        copies[name] = pltpu.make_async_remote_copy(
            src_ref=src,
            dst_ref=dst,
            send_sem=s.ssem.at[n],
            recv_sem=s.rsem.at[n],
            device_id=to[where],
            device_id_type=pl.DeviceIdType.MESH,
        )
        copies[name].start()

    def local(name, src, dst):
        assert name not in copies, name
        n = len(copies)
        copies[name] = pltpu.make_async_copy(src, dst, s.ssem.at[n])
        copies[name].start()

    def got(*names):
        for name in names:
            copies[name].wait_recv()

    def sent(*names):
        for name in names:
            copies[name].wait_send()

    def done(*names):
        for name in names:
            copies[name].wait()

    def add(dst, src):
        dst[...] = (dst[...].astype(F32) + src[...].astype(F32)).astype(BF16)

    def phase(body):
        def run(*args):
            pl.when(r < 4)(functools.partial(body, *args))

        return run

    def w_a(i, lo=0, hi=la):
        return s.WA[i, :, :, :, lo:hi].reshape(d, hi - lo)

    def w_m(i, lo=0, hi=3 * ff):
        return s.WM[i, :, :, :, lo:hi].reshape(d, hi - lo)

    def put(ref, i, lo, value):
        n = value.shape[1]
        ref[i, :, :, :, lo : lo + n] = value.astype(BF16).reshape(4, 2, d // 8, n)

    def grad_m(i):
        return s.WM if isinstance(i, int) and i == 3 else s.GM

    def blocks():
        return [slice(j * C, (j + 1) * C) for j in range(n_blk)]

    def gain(which):
        return s.GAIN[...].reshape(d, s.GAIN.shape[-1])[:, which : which + 1].astype(F32)

    def x_of(sl):
        return s.X[:, :, sl].reshape(d, sl.stop - sl.start).astype(F32)

    @phase
    def setup():
        s.ATT[:, wide:] = jnp.zeros((4, s.ATT.shape[1] - wide, length), BF16)
        s.GG[...] = jnp.zeros(s.GG.shape, F32)
        pos = lax.broadcasted_iota(jnp.int32, (1, length), 1)
        bias = jnp.where(pos < s.lengths[r], 0.0, -1e30)
        shape = (4 * heads, 16, length)
        s.K[:, E:] = jnp.broadcast_to(pack_rows([bias, 1.0, 1.0, 1.0], length), shape)
        s.Q[:, E:] = jnp.broadcast_to(pack_rows([1.0], length), shape)
        s.V[:, E:] = jnp.broadcast_to(pack_rows([1.0, 1.0, 1.0], length), shape)

    @phase
    def norm(which):
        for sl in blocks():
            x = s.MID[:, sl] if which else x_of(sl)
            inv = lax.rsqrt(jnp.sum(x * x, axis=0, keepdims=True) * (1.0 / d) + EPS)
            s.R[which : which + 1, sl] = inv
            (s.N2 if which else s.N1)[:, sl] = (x * inv * gain(which)).astype(BF16)

    def halves():
        return [slice(0, length // 2), slice(length // 2, length)]

    @phase
    def project(i):
        for sl in halves():
            p = dg(w_a(i), s.N1[:, sl], (0, 0))
            cos, sin = s.cos[:, sl], s.sin[:, sl]
            for k in range(heads):
                part = [p[n * wide + k * E : n * wide + (k + 1) * E] for n in (1, 2, 3)]
                s.Q[heads * i + k, :E, sl] = (rope(part[0], cos, sin, 1.0) * (LOG2E / math.sqrt(E))).astype(BF16)
                s.K[heads * i + k, :E, sl] = rope(part[1], cos, sin, 1.0).astype(BF16)
                s.V[heads * i + k, :E, sl] = part[2].astype(BF16)

    def causal():
        return lax.broadcasted_iota(jnp.int32, (C, C), 0) <= lax.broadcasted_iota(jnp.int32, (C, C), 1)

    @phase
    def attend(i):
        tri = causal()
        items = [(k, j) for k in range(heads) for j in range(n_blk)]
        lse = []

        def scores(k, j):
            return dg(s.K[heads * i + k, :, : (j + 1) * C], s.Q[heads * i + k, :, j * C : (j + 1) * C], (0, 0))

        def soft(v, j):
            n = j * C
            diag = jnp.where(tri, v[n:], -1e30)
            top = jnp.max(diag, axis=0, keepdims=True)
            if j:
                top = jnp.maximum(top, jnp.max(v[:n], axis=0, keepdims=True))
            e = jnp.exp2(diag - top).astype(BF16)
            if j:
                e = jnp.concatenate([jnp.exp2(v[:n] - top).astype(BF16), e], axis=0)
            return top, e

        def mix(k, j, top, e):
            sl = slice(j * C, (j + 1) * C)
            o = dg(s.V[heads * i + k, :, : (j + 1) * C], e, (1, 0))
            total = o[E : E + 1]
            s.ATT[i, k * E : (k + 1) * E, sl] = (o[:E] * (1.0 / total)).astype(BF16)
            lse.append((k, sl, pack_rows([1.0, *split3(-(top + jnp.log2(total)))], C)))

        held, now = None, scores(*items[0])
        for n, (k, j) in enumerate(items):
            later = scores(*items[n + 1]) if n + 1 < len(items) else None
            top, e = soft(now, j)
            if held:
                mix(*held)
            held, now = (k, j, top, e), later
        mix(*held)
        for k, sl, rows in lse:
            s.Q[heads * i + k, E:, sl] = rows

    @phase
    def out_project():
        for i in range(4):
            for sl in halves():
                y = dg(w_a(i, 0, s.ATT.shape[1]), s.ATT[i, :, sl], (1, 0))
                s.MID[:, sl] = (s.MID[:, sl] if i else s.X[:, :, sl].reshape(d, length // 2).astype(F32)) + y

    @phase
    def mlp(i, first):

        def dots(sl):
            gu = dg(w_m(i, 0, 2 * ff), s.N2[:, sl], (0, 0))
            return gu, dg(w_m(i, 2 * ff), s.G[:, :, sl].reshape(d, C), (0, 0))

        def mix(sl, gu, d_hid):
            gate, up = gu[:ff], gu[ff:]
            sig = 1.0 / (1.0 + jnp.exp(-gate))
            silu = gate * sig
            s.HD[:ff, sl] = (silu * up).astype(BF16)
            s.HD[ff : 2 * ff, sl] = (d_hid * up * (sig + silu * (1.0 - sig))).astype(BF16)
            s.HD[2 * ff :, sl] = (d_hid * silu).astype(BF16)

        now = dots(blocks()[0])
        for j, sl in enumerate(blocks()):
            later = dots(blocks()[j + 1]) if j + 1 < n_blk else None
            mix(sl, *now)
            now = later
        for sl in halves():
            y = dg(w_m(i, 2 * ff), s.HD[:ff, sl], (1, 0))
            s.FIN[:, sl] = (s.MID if first else s.FIN)[:, sl] + y
            z = dg(w_m(i, 0, 2 * ff), s.HD[ff:, sl], (1, 0))
            s.DN[:, sl] = z if first else s.DN[:, sl] + z

    @phase
    def mlp_grad(i):
        put(grad_m(i), i, 0, dg(s.N2[...], s.HD[ff : 2 * ff], (1, 1)))
        put(grad_m(i), i, ff, dg(s.N2[...], s.HD[2 * ff :], (1, 1)))
        put(grad_m(i), i, 2 * ff, dg(s.G[...].reshape(d, length), s.HD[:ff], (1, 1)))

    @phase
    def norm_back(which, lo, hi):
        total = jnp.zeros((d, 128), F32)
        for j in range(lo, hi, 128):
            sl = slice(j, j + 128)
            dn = (s.DN if which else s.FIN)[:, sl]
            inv = s.R[which : which + 1, sl]
            unit = (s.MID[:, sl] if which else x_of(sl)) * inv
            e = dn * gain(which)
            inner = jnp.sum(e * unit, axis=0, keepdims=True) * (1.0 / d)
            dv = inv * (e - unit * inner)
            total = total + dn * unit
            if which:
                dm = s.G[:, :, sl].reshape(d, 128).astype(F32) + dv
                s.DN[:, sl] = dm
                s.N2[:, sl] = dm.astype(BF16)
            else:
                s.HD[d:, sl] = (s.DN[:, sl] + dv).astype(BF16)
        line = jnp.sum(total.T, axis=0, keepdims=True)
        for k in range(4):
            s.GG[k, which : which + 1, :wide] += line[:, k * wide : (k + 1) * wide]

    dr = E + 16

    @phase
    def attend_back(i, first, part):
        if part != 1:
            d_o = dg(w_a(i, 0, s.ATT.shape[1]), s.N2[...], (0, 0))[:wide].astype(BF16)
            for k in range(heads):
                mine = d_o[k * E : (k + 1) * E]
                s.HD[d + k * dr : d + k * dr + E] = mine
                inner = jnp.sum(mine.astype(F32) * s.ATT[i, k * E : (k + 1) * E].astype(F32), axis=0, keepdims=True)
                s.HD[d + k * dr + E : d + (k + 1) * dr] = pack_rows(split3(-inner), length)
        tri = causal()
        mid = n_blk // 2 if part == 0 else 0
        items = [(k, j) for k in range(heads) for j in range(mid, n_blk if part != 1 else n_blk // 2)]

        def start(k, j):
            n, sl, g = (j + 1) * C, slice(j * C, (j + 1) * C), heads * i + k
            return dg(s.K[g, :, :n], s.Q[g, :, sl], (0, 0)), dg(
                s.V[g, :, :n], s.HD[d + k * dr : d + (k + 1) * dr, sl], (0, 0)
            )

        def finish(k, j, sc, dp):
            n, sl, g = (j + 1) * C, slice(j * C, (j + 1) * C), heads * i + k
            p = jnp.where(tri, jnp.exp2(sc[n - C :]), 0.0)
            if j:
                p = jnp.concatenate([jnp.exp2(sc[: n - C]), p], axis=0)
            ds, p = (p * dp).astype(BF16), p.astype(BF16)
            s.MID[k * E : (k + 1) * E, sl] = dg(s.K[g, :E, :n], ds, (1, 0))
            dk, dv = dg(s.Q[g, :E, sl], ds, (1, 1)), dg(s.HD[d + k * dr : d + k * dr + E, sl], p, (1, 1))
            at = slice(wide + k * E, wide + (k + 1) * E), slice(2 * wide + k * E, 2 * wide + (k + 1) * E)
            if part != 1 and j == mid:
                s.MID[at[0], n:] = jnp.zeros((E, length - n), F32)
                s.MID[at[1], n:] = jnp.zeros((E, length - n), F32)
                s.MID[at[0], :n] = dk
                s.MID[at[1], :n] = dv
            else:
                s.MID[at[0], :n] += dk
                s.MID[at[1], :n] += dv

        now = start(*items[0])
        for n, (k, j) in enumerate(items):
            later = start(*items[n + 1]) if n + 1 < len(items) else None
            finish(k, j, *now)
            now = later
        for sl in halves() if part is None else halves()[1 - part : 2 - part]:
            cos, sin = s.cos[:, sl], s.sin[:, sl]
            dp = [jnp.zeros((wide, length // 2), BF16)]
            for n, scale in enumerate((1.0 / math.sqrt(E), 1.0 / LOG2E, None)):
                for k in range(heads):
                    v = s.MID[n * wide + k * E : n * wide + (k + 1) * E, sl]
                    dp.append((v if scale is None else rope(v * scale, cos, sin, -1.0)).astype(BF16))
            dp = jnp.concatenate(dp, axis=0)
            s.RDM[:2, :, :, sl] = dp.reshape(2, 4, d // 8, length // 2)
            z = dg(w_a(i), dp, (1, 0))
            s.FIN[:, sl] = z if first else s.FIN[:, sl] + z

    @phase
    def attend_grad(i):
        dp = s.RDM[:2, :, :, :length].reshape(d, length)
        gq, go = dg(s.N1[...], dp, (1, 1)), dg(s.N2[...], s.ATT[i], (1, 1))
        n = go.shape[1]
        put(s.WA, i, 0, gq[:, :n] + go)
        put(s.WA, i, n, gq[:, n:])

    def own(ref, lo, hi):
        return ref.at[h, :, lo:hi]

    def spread(name, src, dst):
        for k in (1, 2, 3):
            send(f"{name}{k}", src(row[k]), dst(r), f"r{k}")
        local(f"{name}0", src(r), dst(r))

    def spread_got(name):
        got(*(f"{name}{k}" for k in (1, 2, 3)))
        done(f"{name}0")

    def spread_sent(name):
        sent(*(f"{name}{k}" for k in (1, 2, 3)))

    def piece(tag, slot, at):
        lo, hi = parts[tag]
        if lo < la:
            return s.WA.at[slot, at, h, :, lo:hi]
        return s.WM.at[slot, at, h, :, lo - la : hi - la]

    def gather_z(tag, slot, name, source=None):
        src, dst = source or piece(tag, slot, cc), piece(tag, slot, cc)
        send(f"{tag}z2_{name}", src, dst, "z2")
        send(f"{tag}z1_{name}", src, dst, "z1")

    def gather_z1(tag, slot, name):
        got(f"{tag}z2_{name}")
        send(f"{tag}z12_{name}", piece(tag, slot, col[2]), piece(tag, slot, col[2]), "z1")

    def gathered(tag, name):
        got(f"{tag}z1_{name}", f"{tag}z12_{name}")

    def gather_sent(tag, name):
        sent(*(f"{tag}z{k}_{name}" for k in ("1", "2", "12")))

    def share(tag, ref, slot, name):
        send(f"{tag}d{name}", ref.at[slot, :, h], ref.at[slot, :, h], "dp")

    def landing(tag, i):
        if tag == "M":
            return s.RDM.at[i]
        return s.RDM.at[2, :, :, i * la : (i + 1) * la] if i < 2 else s.RDA.at[i - 2]

    def fold(tag, ref, i):
        got(f"{tag}_fold{i}")
        add(ref.at[i, :, h], landing(tag, i))

    def fold_send(tag, ref, i):
        send(f"{tag}_fold{i}", ref.at[i, :, 1 - h], landing(tag, i), "dp")

    ways = {
        "A": (s.WA, s.RBA, s.RZA, s.RYA, 0, la),
        "M": (s.GM, s.RBM, s.RZM, s.RYM, 0, 2 * ff),
        "N": (s.GM, s.RBN, s.RZN, s.RYN, 2 * ff, lm),
    }

    def spot(tag, slot, at):
        ref, _, _, _, lo, hi = ways[tag]
        if tag != "A":
            ref = grad_m(slot)
        return ref.at[slot, at, h, :, lo:hi]

    def b_send(tag, slot, k):
        at = cc if tag == "N" else slice(None)
        send(f"{tag}_half{k}", spot(tag, slot, at), ways[tag][1].at[k], "b")

    def b_fold(tag, slot, k):
        got(f"{tag}_half{k}")
        add(spot(tag, slot, cc if tag == "N" else slice(None)), ways[tag][1].at[k])

    def z1_send(tag, slot, k):
        send(f"{tag}_far{k}", spot(tag, slot, col[3]), ways[tag][2].at[k, 1], "z1")

    def z2_send(tag, slot, k):
        got(f"{tag}_far{k}")
        add(spot(tag, slot, col[2]), ways[tag][2].at[k, 1])
        send(f"{tag}_last{k}", spot(tag, slot, col[2]), ways[tag][3].at[k], "z2")
        send(f"{tag}_near{k}", spot(tag, slot, col[1]), ways[tag][2].at[k, 0], "z1")

    def z_finish(tag, slot, k):
        got(f"{tag}_near{k}", f"{tag}_last{k}")
        mine = spot(tag, slot, cc)
        mine[...] = (
            mine[...].astype(F32) + ways[tag][2][k, 0].astype(F32) + ways[tag][3][k].astype(F32)
        ).astype(BF16)

    barrier = pltpu.get_barrier_semaphore()
    friends = ("dp", "z1", "z2", "r1", "r2", "r3")
    for name in friends:
        pl.semaphore_signal(barrier, inc=1, device_id=to[name], device_id_type=pl.DeviceIdType.MESH)
    pl.semaphore_wait(barrier, len(friends))

    send("Aa", own(s.w, *parts["A"]), piece("A", a, cc), "a")
    gather_z("A", 0, "0", own(s.w, *parts["A"]))
    send("Ma", own(s.w, *parts["M"]), piece("M", a, cc), "a")
    spread("hid", lambda i: s.hidden.at[i], lambda i: s.X.at[i])
    spread("gain", lambda i: s.gains, lambda i: s.GAIN.at[i])
    local("A0", own(s.w, 0, la), s.WA.at[0, cc, h])
    local("M0", own(s.w, la, la + lm), s.WM.at[0, cc, h])
    setup()
    got("Aa")
    gather_z("A", a, "a")
    gather_z1("A", 0, "0")
    gather_z1("A", a, "a")
    gathered("A", "0")
    done("A0", "M0")
    share("A", s.WA, 0, "0")
    send("Ab0", piece("A", 0, slice(None)), piece("A", b, slice(None)), "b")
    gathered("A", "a")
    share("A", s.WA, a, "a")
    got("Ma")
    gather_z("M", a, "a")
    spread_got("hid")
    spread_got("gain")
    norm(0)
    got("Ad0")
    project(0)
    gather_z("M", 0, "0")
    attend(0)
    got("Ab0")
    share("A", s.WA, b, "b")
    send("Aba", piece("A", a, slice(None)), piece("A", 3, slice(None)), "b")
    spread("cot", lambda i: s.cot.at[i], lambda i: s.G.at[i])
    got("Ada", "Adb")
    project(1)
    attend(1)
    gather_z1("M", a, "a")
    project(2)
    attend(2)
    got("Aba")
    share("A", s.WA, 3, "3")
    got("Ad3")
    project(3)
    attend(3)
    gather_z1("M", 0, "0")
    out_project()
    gathered("M", "a")
    share("M", s.WM, a, "a")
    send("Mba", piece("M", a, slice(None)), piece("M", 3, slice(None)), "b")
    norm(1)
    gathered("M", "0")
    share("M", s.WM, 0, "0")
    spread_got("cot")
    got("Md0")
    mlp(0, True)
    mlp_grad(0)
    fold_send("M", s.GM, 0)
    got("Mba")
    share("M", s.WM, 3, "3")
    send("Mb0", piece("M", 0, slice(None)), piece("M", b, slice(None)), "b")
    fold("M", s.GM, 0)
    z1_send("N", 0, 0)
    got("Md3")
    mlp(3, False)
    z2_send("N", 0, 0)
    sent("Md3")
    mlp_grad(3)
    fold_send("M", s.WM, 3)
    z_finish("N", 0, 0)
    fold("M", s.WM, 3)
    b_send("M", 3, 1)
    z1_send("N", 3, 3)
    got("Mb0")
    share("M", s.WM, b, "b")
    got("Mda", "Mdb")
    mlp(1, False)
    z2_send("N", 3, 3)
    mlp_grad(1)
    fold_send("M", s.GM, 1)
    mlp(2, False)
    fold("M", s.GM, 1)
    z1_send("N", 1, 1)
    z_finish("N", 3, 3)
    mlp_grad(2)
    fold_send("M", s.GM, 2)
    z2_send("N", 1, 1)
    spread_sent("cot")
    s.HD[:d] = s.FIN[...].astype(BF16)
    norm_back(1, 0, length)
    fold("M", s.GM, 2)
    b_send("M", b, 0)
    z1_send("N", 2, 2)
    b_fold("M", a, 1)
    z1_send("M", a, 1)
    gather_sent("A", "0")
    gather_sent("A", "a")
    sent("Ad0", "Ada", "Adb", "Ad3", "Aa", "Ab0", "Aba")
    attend_back(3, True, None)
    z_finish("N", 1, 1)
    z2_send("N", 2, 2)
    z2_send("M", a, 1)
    for k in (1, 2, 3):
        send(f"out{k}", s.HD.at[pl.ds(pl.multiple_of(row[k] * wide, wide), wide)], s.out.at[r], f"r{k}")
    local("out0", s.HD.at[pl.ds(pl.multiple_of(r * wide, wide), wide)], s.out.at[r])
    attend_grad(3)
    fold_send("A", s.WA, 3)
    b_fold("M", 0, 0)
    z1_send("M", 0, 0)
    fold("A", s.WA, 3)
    b_send("A", 3, 1)
    attend_back(1, False, None)
    z_finish("N", 2, 2)
    b_send("N", b, 0)
    b_send("N", 3, 1)
    z2_send("M", 0, 0)
    attend_grad(1)
    fold_send("A", s.WA, 1)
    z_finish("M", a, 1)
    fold("A", s.WA, 1)
    attend_back(2, False, None)
    b_fold("N", a, 1)
    send("Me", s.GM.at[a, cc, h], s.REM, "a")
    attend_grad(2)
    fold_send("A", s.WA, 2)
    z_finish("M", 0, 0)
    b_fold("N", 0, 0)
    fold("A", s.WA, 2)
    b_send("A", b, 0)
    b_fold("A", a, 1)
    z1_send("A", a, 1)
    attend_back(0, False, 0)
    z2_send("A", a, 1)
    norm_back(0, length // 2, length)

    def dx(k, part):
        at, sl = r if k == 0 else row[k], halves()[part]
        return s.HD.at[pl.ds(pl.multiple_of(d + at * wide, wide), wide), sl], s.dx.at[r, :, sl]

    for k in (1, 2, 3):
        send(f"dx{k}_1", *dx(k, 1), f"r{k}")
    local("dx0_1", *dx(0, 1))
    attend_back(0, False, 1)
    attend_grad(0)
    fold_send("A", s.WA, 0)
    norm_back(0, 0, length // 2)
    for k in (1, 2, 3):
        send(f"gg{k}", s.GG.at[row[k]], s.RG.at[k - 1], f"r{k}")
    b_fold("A", 0, 0)
    fold("A", s.WA, 0)
    z1_send("A", 0, 0)
    z_finish("A", a, 1)
    send("Ae", s.WA.at[a, cc, h], s.REA, "a")
    for k in (1, 2, 3):
        send(f"dx{k}_0", *dx(k, 0), f"r{k}")
    local("dx0_0", *dx(0, 0))
    got("Me")
    add(s.GM.at[0, cc, h], s.REM)
    send("Mf", s.GM.at[0, cc, h], s.grads.at[h, :, la:], "dp")
    local("Mf0", s.GM.at[0, cc, h], s.grads.at[h, :, la:])
    got("gg1", "gg2", "gg3")
    s.GS[0] = (s.GG[r] + s.RG[0]) + (s.RG[1] + s.RG[2])
    send("gg4", s.GS.at[0], s.RG.at[3], "z1")
    z2_send("A", 0, 0)
    got("gg4")
    s.GS[1] = s.GS[0] + s.RG[3]
    send("gg5", s.GS.at[1], s.RG.at[4], "z2")
    got("Ae")
    got("gg5")
    s.GS[2] = s.GS[1] + s.RG[4]
    send("gg6", s.GS.at[2], s.RG.at[5], "dp")
    z_finish("A", 0, 0)
    add(s.WA.at[0, cc, h], s.REA)
    send("Af", s.WA.at[0, cc, h], s.grads.at[h, :, :la], "dp")
    local("Af0", s.WA.at[0, cc, h], s.grads.at[h, :, :la])
    got("gg6")
    s.GS[3] = s.GS[2] + s.RG[5]
    local("gg", s.GS.at[3], s.gain_grads)
    done("gg", "Mf0", "Af0", "out0", "dx0_0", "dx0_1")
    got("Mf", "Af")
    for name in ("out{}", "dx{}_0", "dx{}_1"):
        got(*(name.format(k) for k in (1, 2, 3)))
        sent(*(name.format(k) for k in (1, 2, 3)))
    spread_sent("hid")
    spread_sent("gain")
    sent("Ma", "Me", "Mf", "Ae", "Af", *(f"gg{n}" for n in range(1, 7)))
    gather_sent("M", "0")
    gather_sent("M", "a")
    sent("Md0", "Mda", "Mdb", "Mb0", "Mba")
    for tag, count in (("A", 2), ("M", 2), ("N", 4)):
        sent(*(f"{tag}_half{k}" for k in (0, 1)))
        sent(*(f"{tag}_{kind}{k}" for kind in ("far", "near", "last") for k in range(count)))
    sent(*(f"{tag}_fold{i}" for tag in "AM" for i in range(4)))


class Refs:
    def __init__(self, names, refs):
        self.__dict__.update(zip(names, refs, strict=True))


INPUTS = ("lengths", "hidden", "cot", "w", "gains", "cos", "sin")
OUTPUTS = ("out", "dx", "grads", "gain_grads")


def shards(groups, hidden, lengths, w_qkv, w_out, w_gate_up, w_down, gain_attn, gain_mlp, cotangent):
    _, wide, length = hidden.shape
    d, ff = 4 * wide, w_gate_up.shape[2]
    rows = w_qkv.shape[0]
    w = jnp.concatenate(
        [w_out.T, w_qkv.reshape(rows, 3 * wide), w_gate_up.reshape(rows, 2 * ff), w_down.T], axis=1
    )
    cols = lax.axis_size("col")
    clubs = [[g * groups + i for i in range(groups)] for g in range(cols // groups)]
    if groups > 1:
        w = lax.all_gather(w, "col", axis_index_groups=clubs, axis=0, tiled=True)
    la, lm, eighth = 4 * wide, 3 * ff, d // 8
    lane = lax.broadcasted_iota(jnp.int32, (wide, 128), 1)
    gains = jnp.where(lane == 0, gain_attn[:, None], gain_mlp[:, None])
    freq = np.exp(np.arange(E // 2, dtype=np.float32) * np.float32(-2.0 * math.log(10000.0) / E))
    angles = freq[:, None] * np.arange(length, dtype=np.float32)[None, :]
    heads = d // E
    scratch = {
        "WA": pltpu.VMEM((4, 4, 2, eighth, la), BF16),
        "WM": pltpu.VMEM((4, 4, 2, eighth, lm), BF16),
        "GM": pltpu.VMEM((3, 4, 2, eighth, lm), BF16),
        "X": pltpu.VMEM((4, wide, length), BF16),
        "G": pltpu.VMEM((4, wide, length), BF16),
        "GAIN": pltpu.VMEM((4, wide, 128), BF16),
        "N1": pltpu.VMEM((d, length), BF16),
        "N2": pltpu.VMEM((d, length), BF16),
        "Q": pltpu.VMEM((heads, E + 16, length), BF16),
        "K": pltpu.VMEM((heads, E + 16, length), BF16),
        "V": pltpu.VMEM((heads, E + 16, length), BF16),
        "ATT": pltpu.VMEM((4, 256, length), BF16),
        "MID": pltpu.VMEM((d, length), F32),
        "FIN": pltpu.VMEM((d, length), F32),
        "DN": pltpu.VMEM((d, length), F32),
        "HD": pltpu.VMEM((3 * ff, length), BF16),
        "R": pltpu.VMEM((8, length), F32),
        "GG": pltpu.VMEM((4, 8, 256), F32),
        "RG": pltpu.VMEM((6, 8, 256), F32),
        "GS": pltpu.VMEM((4, 8, 256), F32),
        "RDA": pltpu.VMEM((2, 4, eighth, la), BF16),
        "RDM": pltpu.VMEM((4, 4, eighth, lm), BF16),
        "RBA": pltpu.VMEM((2, 4, eighth, la), BF16),
        "RBM": pltpu.VMEM((2, 4, eighth, 2 * ff), BF16),
        "RBN": pltpu.VMEM((2, eighth, ff), BF16),
        "RZA": pltpu.VMEM((2, 2, eighth, la), BF16),
        "RZM": pltpu.VMEM((2, 2, eighth, 2 * ff), BF16),
        "RZN": pltpu.VMEM((4, 2, eighth, ff), BF16),
        "RYA": pltpu.VMEM((2, eighth, la), BF16),
        "RYM": pltpu.VMEM((2, eighth, 2 * ff), BF16),
        "RYN": pltpu.VMEM((4, eighth, ff), BF16),
        "REA": pltpu.VMEM((eighth, la), BF16),
        "REM": pltpu.VMEM((eighth, lm), BF16),
        "ssem": pltpu.SemaphoreType.DMA((N_COPIES,)),
        "rsem": pltpu.SemaphoreType.DMA((N_COPIES,)),
    }

    def kernel(*refs):
        layer(groups, Refs((*INPUTS, *OUTPUTS, *scratch), refs))

    anywhere, vmem = pl.BlockSpec(memory_space=pl.ANY), pl.BlockSpec(memory_space=pltpu.VMEM)
    out, dx, grad, gain_grads = pl.pallas_call(
        kernel,
        out_shape=(
            jax.ShapeDtypeStruct(hidden.shape, BF16),
            jax.ShapeDtypeStruct(hidden.shape, BF16),
            jax.ShapeDtypeStruct((2, eighth, la + lm), BF16),
            jax.ShapeDtypeStruct((8, 256), F32),
        ),
        in_specs=[pl.BlockSpec(memory_space=pltpu.SMEM), *[anywhere] * 4, vmem, vmem],
        out_specs=(anywhere,) * 4,
        scratch_shapes=list(scratch.values()),
        compiler_params=pltpu.CompilerParams(
            collective_id=0, has_side_effects=True, vmem_limit_bytes=63 * 2**20
        ),
    )(lengths, hidden, cotangent, w.reshape(2, eighth, la + lm), gains, np.cos(angles), np.sin(angles))
    grad = grad.reshape(d // 4, la + lm)
    if groups > 1:
        grad = lax.psum_scatter(grad, "col", axis_index_groups=clubs, scatter_dimension=0, tiled=True)
        gain_grads = lax.psum(gain_grads, "col", axis_index_groups=clubs)
    out, dx, g_qkv, g_out, g_gu, g_down, g_one, g_two = finish(out, dx, grad, gain_grads, wide, ff)
    return (out, dx, g_qkv.transpose(1, 0, 2), g_out, g_gu, g_down.T, g_one, g_two)


def finish(out, dx, grad, gain_grads, wide, ff):
    n, _, length = out.shape
    rows = grad.shape[0]

    def kernel(out_in, dx_in, grad_in, gain_in, out_ref, dx_ref, qkv_ref, back_ref, gu_ref, down_ref, one_ref, two_ref):
        out_ref[...] = out_in[...]
        dx_ref[...] = dx_in[...].astype(F32)

        @pl.when(pl.program_id(0) == 0)
        def _():
            g = grad_in[...].astype(F32)
            back_ref[...] = g[:, :wide].T
            for k in range(3):
                qkv_ref[k] = g[:, (k + 1) * wide : (k + 2) * wide]
            for k in range(2):
                gu_ref[:, k, :] = g[:, 4 * wide + k * ff : 4 * wide + (k + 1) * ff]
            down_ref[...] = g[:, 4 * wide + 2 * ff :]
            one_ref[...] = gain_in[0, :wide]
            two_ref[...] = gain_in[1, :wide]

    def block(*shape):
        return pl.BlockSpec(shape, lambda i: (0,) * len(shape))

    tokens = pl.BlockSpec((1, wide, length), lambda i: (i, 0, 0))
    shapes = ((3, rows, wide), (wide, rows), (rows, 2, ff), (rows, ff), (wide,), (wide,))
    return pl.pallas_call(
        kernel,
        grid=(n,),
        out_shape=(
            jax.ShapeDtypeStruct(out.shape, BF16),
            jax.ShapeDtypeStruct(out.shape, F32),
            *(jax.ShapeDtypeStruct(shape, F32) for shape in shapes),
        ),
        in_specs=[tokens, tokens, block(*grad.shape), block(*gain_grads.shape)],
        out_specs=(tokens, tokens, *(block(*shape) for shape in shapes)),
        compiler_params=pltpu.CompilerParams(vmem_limit_bytes=60 * 2**20),
    )(out, dx, grad, gain_grads)


def solution(mesh):
    tokens, wide = P(("dp", "col"), "row", None), P("col", None, "row")
    back, gain = P("row", "col"), P("row")
    return jax.shard_map(
        functools.partial(shards, mesh.shape["col"] // 4),
        mesh=mesh,
        in_specs=(tokens, P(("dp", "col")), wide, back, wide, back, gain, gain, tokens),
        out_specs=(tokens, tokens, wide, back, wide, back, gain, gain),
        check_vma=False,
    )
```

```python
import functools
import math

import jax
import jax.numpy as jnp
import numpy as np
from jax import lax
from jax.experimental import pallas as pl
from jax.experimental.pallas import tpu as pltpu
from jax.sharding import PartitionSpec as P

EPS = 1e-05
E = 64
C = 256
LOG2E = math.log2(math.e)
F32, BF16 = jnp.float32, jnp.bfloat16
N_COPIES = 128


def dg(a, b, contract):
    return lax.dot_general(a, b, ((contract[:1], contract[1:]), ((), ())), preferred_element_type=F32)


def rope(v, cos, sin, sign):
    half = v.shape[0] // 2
    a, b = v[:half], v[half:]
    return jnp.concatenate([a * cos - sign * (b * sin), b * cos + sign * (a * sin)], axis=0)


def pack_rows(values, width):
    row = lax.broadcasted_iota(jnp.int32, (16, width), 0)
    out = jnp.zeros((16, width), F32)
    for i, v in enumerate(values):
        out = jnp.where(row == i, v, out)
    return out.astype(BF16)


def split3(v):
    hi = v.astype(BF16).astype(F32)
    mid = (v - hi).astype(BF16).astype(F32)
    return hi, mid, v - hi - mid


def layer(groups, refs):
    s = refs
    d, length = s.N1.shape
    wide = s.X.shape[1]
    heads = wide // E
    ff = s.HD.shape[0] // 3
    la, lm = 4 * wide, 3 * ff
    n_blk = length // C

    h, r, c = lax.axis_index("dp"), lax.axis_index("row"), lax.axis_index("col")
    cc, ci = c // groups, c % groups
    col = {1: cc + 1 - 2 * (cc % 2), 2: (cc + 2) % 4, 3: 3 - cc}
    row = {1: r + 1 - 2 * (r % 2), 2: (r + 2) % 4, 3: 3 - r}
    a, b = 1 + h, 2 - h
    to = {
        "dp": {"dp": 1 - h},
        "z1": {"col": col[1] * groups + ci},
        "z2": {"col": col[2] * groups + ci},
        "r1": {"row": row[1]},
        "r2": {"row": row[2]},
        "r3": {"row": row[3]},
        "z3": {"col": col[3] * groups + ci},
        "a": {"row": (1 - h) * row[1] + h * row[2]},
        "b": {"row": (1 - h) * row[2] + h * row[1]},
    }
    copies = {}
    parts = {"A": (0, la), "M": (la, la + lm)}

    def send(name, src, dst, where):
        assert name not in copies, name
        n = len(copies)
        copies[name] = pltpu.make_async_remote_copy(
            src_ref=src,
            dst_ref=dst,
            send_sem=s.ssem.at[n],
            recv_sem=s.rsem.at[n],
            device_id=to[where],
            device_id_type=pl.DeviceIdType.MESH,
        )
        copies[name].start()

    def local(name, src, dst):
        assert name not in copies, name
        n = len(copies)
        copies[name] = pltpu.make_async_copy(src, dst, s.ssem.at[n])
        copies[name].start()

    def got(*names):
        for name in names:
            copies[name].wait_recv()

    def sent(*names):
        for name in names:
            copies[name].wait_send()

    def done(*names):
        for name in names:
            copies[name].wait()

    def add(dst, src):
        dst[...] = (dst[...].astype(F32) + src[...].astype(F32)).astype(BF16)

    def phase(body):
        def run(*args):
            pl.when(r < 4)(functools.partial(body, *args))

        return run

    def w_a(i, lo=0, hi=la):
        return s.WA[i, :, :, :, lo:hi].reshape(d, hi - lo)

    def w_m(i, lo=0, hi=3 * ff):
        return s.WM[i, :, :, :, lo:hi].reshape(d, hi - lo)

    def put(ref, i, lo, value):
        n = value.shape[1]
        ref[i, :, :, :, lo : lo + n] = value.astype(BF16).reshape(4, 2, d // 8, n)

    def grad_m(i):
        return s.WM if isinstance(i, int) and i == 3 else s.GM

    def blocks():
        return [slice(j * C, (j + 1) * C) for j in range(n_blk)]

    def gain(which):
        return s.GC[:, which : which + 1]

    @phase
    def gain_columns():
        for k in range(4):
            turned = jnp.concatenate([s.GAIN[k].astype(F32)] * 8, axis=0).T
            s.GC[k * wide : (k + 1) * wide] = turned[:wide]

    def x_of(sl):
        return s.X[:, :, sl].reshape(d, sl.stop - sl.start).astype(F32)

    @phase
    def setup():
        s.ATT[:, wide:] = jnp.zeros((4, s.ATT.shape[1] - wide, length), BF16)
        s.GG[...] = jnp.zeros(s.GG.shape, F32)
        pos = lax.broadcasted_iota(jnp.int32, (1, length), 1)
        bias = jnp.where(pos < s.lengths[r], 0.0, -1e30)
        shape = (4 * heads, 16, length)
        s.K[:, E:] = jnp.broadcast_to(pack_rows([bias, 1.0, 1.0, 1.0], length), shape)
        s.Q[:, E:] = jnp.broadcast_to(pack_rows([1.0], length), shape)
        s.V[:, E:] = jnp.broadcast_to(pack_rows([1.0, 1.0, 1.0], length), shape)

    @phase
    def norm(which):
        for sl in blocks():
            x = s.MID[:, sl] if which else x_of(sl)
            inv = lax.rsqrt(jnp.sum(x * x, axis=0, keepdims=True) * (1.0 / d) + EPS)
            s.R[which : which + 1, sl] = inv
            (s.N2 if which else s.N1)[:, sl] = (x * inv * gain(which)).astype(BF16)

    def halves():
        return [slice(0, length // 2), slice(length // 2, length)]

    @phase
    def project(i):
        for sl in halves():
            p = dg(w_a(i), s.N1[:, sl], (0, 0))
            cos, sin = s.cos[:, sl], s.sin[:, sl]
            for k in range(heads):
                part = [p[n * wide + k * E : n * wide + (k + 1) * E] for n in (1, 2, 3)]
                s.Q[heads * i + k, :E, sl] = (rope(part[0], cos, sin, 1.0) * (LOG2E / math.sqrt(E))).astype(BF16)
                s.K[heads * i + k, :E, sl] = rope(part[1], cos, sin, 1.0).astype(BF16)
                s.V[heads * i + k, :E, sl] = part[2].astype(BF16)

    def causal():
        return lax.broadcasted_iota(jnp.int32, (C, C), 0) <= lax.broadcasted_iota(jnp.int32, (C, C), 1)

    @phase
    def attend(i):
        tri = causal()
        items = [(k, j) for k in range(heads) for j in range(n_blk)]
        lse = []

        def scores(k, j):
            return dg(s.K[heads * i + k, :, : (j + 1) * C], s.Q[heads * i + k, :, j * C : (j + 1) * C], (0, 0))

        def soft(v, j):
            n = j * C
            diag = jnp.where(tri, v[n:], -1e30)
            top = jnp.max(diag, axis=0, keepdims=True)
            if j:
                top = jnp.maximum(top, jnp.max(v[:n], axis=0, keepdims=True))
            e = jnp.exp2(diag - top).astype(BF16)
            if j:
                e = jnp.concatenate([jnp.exp2(v[:n] - top).astype(BF16), e], axis=0)
            return top, e

        def mix(k, j, top, e):
            sl = slice(j * C, (j + 1) * C)
            o = dg(s.V[heads * i + k, :, : (j + 1) * C], e, (1, 0))
            total = o[E : E + 1]
            s.ATT[i, k * E : (k + 1) * E, sl] = (o[:E] * (1.0 / total)).astype(BF16)
            lse.append((k, sl, pack_rows([1.0, *split3(-(top + jnp.log2(total)))], C)))

        held, now = None, scores(*items[0])
        for n, (k, j) in enumerate(items):
            later = scores(*items[n + 1]) if n + 1 < len(items) else None
            top, e = soft(now, j)
            if held:
                mix(*held)
            held, now = (k, j, top, e), later
        mix(*held)
        for k, sl, rows in lse:
            s.Q[heads * i + k, E:, sl] = rows

    @phase
    def out_project():
        for i in range(4):
            for sl in halves():
                y = dg(w_a(i, 0, s.ATT.shape[1]), s.ATT[i, :, sl], (1, 0))
                s.MID[:, sl] = (s.MID[:, sl] if i else s.X[:, :, sl].reshape(d, length // 2).astype(F32)) + y

    @phase
    def mlp(i):

        def dots(sl):
            gu = dg(w_m(i, 0, 2 * ff), s.N2[:, sl], (0, 0))
            return gu, dg(w_m(i, 2 * ff), s.G[:, :, sl].reshape(d, C), (0, 0))

        def mix(sl, gu, d_hid):
            gate, up = gu[:ff], gu[ff:]
            sig = 1.0 / (1.0 + jnp.exp(-gate))
            silu = gate * sig
            s.HD[:ff, sl] = (silu * up).astype(BF16)
            s.HD[ff : 2 * ff, sl] = (d_hid * up * (sig + silu * (1.0 - sig))).astype(BF16)
            s.HD[2 * ff :, sl] = (d_hid * silu).astype(BF16)

        now = dots(blocks()[0])
        for j, sl in enumerate(blocks()):
            later = dots(blocks()[j + 1]) if j + 1 < n_blk else None
            mix(sl, *now)
            now = later

    @phase
    def mlp_out(i, first):
        for sl in halves():
            y = dg(w_m(i, 2 * ff), s.HD[:ff, sl], (1, 0))
            s.FIN[:, sl] = (s.MID if first else s.FIN)[:, sl] + y
            z = dg(w_m(i, 0, 2 * ff), s.HD[ff:, sl], (1, 0))
            s.DN[:, sl] = z if first else s.DN[:, sl] + z

    @phase
    def mlp_grad(i):
        put(grad_m(i), i, 0, dg(s.N2[...], s.HD[ff : 2 * ff], (1, 1)))
        put(grad_m(i), i, ff, dg(s.N2[...], s.HD[2 * ff :], (1, 1)))
        put(grad_m(i), i, 2 * ff, dg(s.G[...].reshape(d, length), s.HD[:ff], (1, 1)))

    @phase
    def norm_back(which, lo, hi):
        total = jnp.zeros((d, 128), F32)
        for j in range(lo, hi, 128):
            sl = slice(j, j + 128)
            dn = (s.DN if which else s.FIN)[:, sl]
            inv = s.R[which : which + 1, sl]
            unit = (s.MID[:, sl] if which else x_of(sl)) * inv
            e = dn * gain(which)
            inner = jnp.sum(e * unit, axis=0, keepdims=True) * (1.0 / d)
            dv = inv * (e - unit * inner)
            total = total + dn * unit
            if which:
                dm = s.G[:, :, sl].reshape(d, 128).astype(F32) + dv
                s.DN[:, sl] = dm
                s.N2[:, sl] = dm.astype(BF16)
            else:
                s.HD[d:, sl] = (s.DN[:, sl] + dv).astype(BF16)
        line = jnp.sum(total.T, axis=0, keepdims=True)
        for k in range(4):
            s.GG[k, which : which + 1, :wide] += line[:, k * wide : (k + 1) * wide]

    dr = E + 16

    @phase
    def attend_back(i, first, part):
        if part != 1:
            d_o = dg(w_a(i, 0, s.ATT.shape[1]), s.N2[...], (0, 0))[:wide].astype(BF16)
            for k in range(heads):
                mine = d_o[k * E : (k + 1) * E]
                s.HD[d + k * dr : d + k * dr + E] = mine
                inner = jnp.sum(mine.astype(F32) * s.ATT[i, k * E : (k + 1) * E].astype(F32), axis=0, keepdims=True)
                s.HD[d + k * dr + E : d + (k + 1) * dr] = pack_rows(split3(-inner), length)
        tri = causal()
        mid = n_blk // 2 if part == 0 else 0
        items = [(k, j) for k in range(heads) for j in range(mid, n_blk if part != 1 else n_blk // 2)]

        def start(k, j):
            n, sl, g = (j + 1) * C, slice(j * C, (j + 1) * C), heads * i + k
            return dg(s.K[g, :, :n], s.Q[g, :, sl], (0, 0)), dg(
                s.V[g, :, :n], s.HD[d + k * dr : d + (k + 1) * dr, sl], (0, 0)
            )

        def finish(k, j, sc, dp):
            n, sl, g = (j + 1) * C, slice(j * C, (j + 1) * C), heads * i + k
            p = jnp.where(tri, jnp.exp2(sc[n - C :]), 0.0)
            if j:
                p = jnp.concatenate([jnp.exp2(sc[: n - C]), p], axis=0)
            ds, p = (p * dp).astype(BF16), p.astype(BF16)
            s.MID[k * E : (k + 1) * E, sl] = dg(s.K[g, :E, :n], ds, (1, 0))
            dk, dv = dg(s.Q[g, :E, sl], ds, (1, 1)), dg(s.HD[d + k * dr : d + k * dr + E, sl], p, (1, 1))
            at = slice(wide + k * E, wide + (k + 1) * E), slice(2 * wide + k * E, 2 * wide + (k + 1) * E)
            if part != 1 and j == mid:
                s.MID[at[0], n:] = jnp.zeros((E, length - n), F32)
                s.MID[at[1], n:] = jnp.zeros((E, length - n), F32)
                s.MID[at[0], :n] = dk
                s.MID[at[1], :n] = dv
            else:
                s.MID[at[0], :n] += dk
                s.MID[at[1], :n] += dv

        now = start(*items[0])
        for n, (k, j) in enumerate(items):
            later = start(*items[n + 1]) if n + 1 < len(items) else None
            finish(k, j, *now)
            now = later
        for sl in halves() if part is None else halves()[1 - part : 2 - part]:
            cos, sin = s.cos[:, sl], s.sin[:, sl]
            dp = [jnp.zeros((wide, length // 2), BF16)]
            for n, scale in enumerate((1.0 / math.sqrt(E), 1.0 / LOG2E, None)):
                for k in range(heads):
                    v = s.MID[n * wide + k * E : n * wide + (k + 1) * E, sl]
                    dp.append((v if scale is None else rope(v * scale, cos, sin, -1.0)).astype(BF16))
            dp = jnp.concatenate(dp, axis=0)
            s.RDM[:2, :, :, sl] = dp.reshape(2, 4, d // 8, length // 2)
            z = dg(w_a(i), dp, (1, 0))
            s.FIN[:, sl] = z if first else s.FIN[:, sl] + z

    @phase
    def attend_grad(i):
        dp = s.RDM[:2, :, :, :length].reshape(d, length)
        gq, go = dg(s.N1[...], dp, (1, 1)), dg(s.N2[...], s.ATT[i], (1, 1))
        n = go.shape[1]
        put(s.WA, i, 0, gq[:, :n] + go)
        put(s.WA, i, n, gq[:, n:])

    def own(ref, lo, hi):
        return ref.at[h, :, lo:hi]

    def spread(name, src, dst):
        for k in (1, 2, 3):
            send(f"{name}{k}", src(row[k]), dst(r), f"r{k}")
        local(f"{name}0", src(r), dst(r))

    def spread_got(name):
        got(*(f"{name}{k}" for k in (1, 2, 3)))
        done(f"{name}0")

    def spread_sent(name):
        sent(*(f"{name}{k}" for k in (1, 2, 3)))

    def piece(tag, slot, at):
        lo, hi = parts[tag]
        if lo < la:
            return s.WA.at[slot, at, h, :, lo:hi]
        return s.WM.at[slot, at, h, :, lo - la : hi - la]

    def gather_z(tag, slot, name, source=None):
        src, dst = source or piece(tag, slot, cc), piece(tag, slot, cc)
        send(f"{tag}z2_{name}", src, dst, "z2")
        send(f"{tag}z1_{name}", src, dst, "z1")

    def gather_z1(tag, slot, name):
        got(f"{tag}z2_{name}")
        send(f"{tag}z12_{name}", piece(tag, slot, col[2]), piece(tag, slot, col[2]), "z1")

    def gathered(tag, name):
        got(f"{tag}z1_{name}", f"{tag}z12_{name}")

    def gather_sent(tag, name):
        sent(*(f"{tag}z{k}_{name}" for k in ("1", "2", "12")))

    def share(tag, ref, slot, name, at=slice(None)):
        send(f"{tag}d{name}", ref.at[slot, at, h], ref.at[slot, at, h], "dp")

    def landing(tag, i):
        if tag == "M":
            return s.RDM.at[i]
        n = (3, 1, 2, 0).index(i)
        return s.RDM.at[2 + n // 2, :, :, n % 2 * la : (n % 2 + 1) * la]

    def fold(tag, ref, i):
        got(f"{tag}_fold{i}")
        add(ref.at[i, :, h], landing(tag, i))

    def fold_send(tag, ref, i):
        send(f"{tag}_fold{i}", ref.at[i, :, 1 - h], landing(tag, i), "dp")

    ways = {
        "A": (s.WA, s.RBA, s.RZA, s.RYA, 0, la),
        "M": (s.GM, s.RBM, s.RZM, s.RYM, 0, lm // 2),
        "N": (s.GM, s.RBN, s.RZN, s.RYN, lm // 2, lm),
    }

    def spot(tag, slot, at):
        ref, _, _, _, lo, hi = ways[tag]
        if tag != "A":
            ref = grad_m(slot)
        return ref.at[slot, at, h, :, lo:hi]

    def b_send(tag, slot, k):
        at = cc if tag == "N" else slice(None)
        send(f"{tag}_half{k}", spot(tag, slot, at), ways[tag][1].at[k], "b")

    def b_fold(tag, slot, k):
        got(f"{tag}_half{k}")
        add(spot(tag, slot, cc if tag == "N" else slice(None)), ways[tag][1].at[k])

    def z1_send(tag, slot, k):
        send(f"{tag}_far{k}", spot(tag, slot, col[3]), ways[tag][2].at[k, 1], "z1")

    def z2_send(tag, slot, k):
        got(f"{tag}_far{k}")
        add(spot(tag, slot, col[2]), ways[tag][2].at[k, 1])
        send(f"{tag}_last{k}", spot(tag, slot, col[2]), ways[tag][3].at[k], "z2")
        send(f"{tag}_near{k}", spot(tag, slot, col[1]), ways[tag][2].at[k, 0], "z1")

    def z_finish(tag, slot, k):
        got(f"{tag}_near{k}", f"{tag}_last{k}")
        mine = spot(tag, slot, cc)
        mine[...] = (
            mine[...].astype(F32) + ways[tag][2][k, 0].astype(F32) + ways[tag][3][k].astype(F32)
        ).astype(BF16)

    barrier = pltpu.get_barrier_semaphore()
    friends = ("dp", "z1", "z2", "z3", "r1", "r2", "r3")
    for name in friends:
        pl.semaphore_signal(barrier, inc=1, device_id=to[name], device_id_type=pl.DeviceIdType.MESH)
    pl.semaphore_wait(barrier, len(friends))

    both = (("", slice(0, 2)), ("'", slice(2, 4)))
    send("Aa", own(s.w, *parts["A"]), piece("A", a, cc), "a")
    gather_z("A", 0, "0", own(s.w, *parts["A"]))
    send("Ma", own(s.w, *parts["M"]), piece("M", a, cc), "a")
    spread("hid", lambda i: s.hidden.at[i], lambda i: s.X.at[i])
    spread("gain", lambda i: s.gains, lambda i: s.GAIN.at[i])
    local("A0", own(s.w, 0, la), s.WA.at[0, cc, h])
    local("M0", own(s.w, la, la + lm), s.WM.at[0, cc, h])
    setup()
    got("Aa")
    gather_z("A", a, "a")
    gather_z1("A", 0, "0")
    gather_z1("A", a, "a")
    gathered("A", "0")
    done("A0", "M0")
    share("A", s.WA, 0, "0")
    send("Ab0", piece("A", 0, slice(None)), piece("A", b, slice(None)), "b")
    gathered("A", "a")
    share("A", s.WA, a, "a")
    send("Aba", piece("A", a, slice(None)), piece("A", 3, slice(None)), "b")
    gather_z("M", 0, "0")
    spread_got("hid")
    spread("cot", lambda i: s.cot.at[i], lambda i: s.G.at[i])
    spread_got("gain")
    gain_columns()
    norm(0)
    got("Ad0")
    project(0)
    attend(0)
    gather_z1("M", 0, "0")
    got("Ma")
    gather_z("M", a, "a")
    got("Ab0")
    share("A", s.WA, b, "b")
    got("Ada", "Adb")
    project(1)
    attend(1)
    project(2)
    got("Aba")
    share("A", s.WA, 3, "3")
    attend(2)
    got("Ad3")
    project(3)
    attend(3)
    gathered("M", "0")
    share("M", s.WM, 0, "0")
    for tick, at in both:
        send(f"Mb0{tick}", piece("M", 0, at), piece("M", b, at), "b")
    gather_z1("M", a, "a")
    out_project()
    norm(1)
    got("Md0")
    spread_got("cot")
    mlp(0)
    mlp_out(0, True)
    gathered("M", "a")
    share("M", s.WM, a, "a")
    send("Mba", piece("M", a, slice(None)), piece("M", 3, slice(None)), "b")
    mlp_grad(0)
    fold_send("M", s.GM, 0)
    for tick, at in both:
        got(f"Mb0{tick}")
        share("M", s.WM, b, f"b{tick}", at)
    fold("M", s.GM, 0)
    z1_send("N", 0, 0)
    got("Mda", "Mdb", "Mdb'")
    mlp(1)
    mlp_out(1, False)
    z2_send("N", 0, 0)
    mlp_grad(1)
    fold_send("M", s.GM, 1)
    mlp(2)
    fold("M", s.GM, 1)
    z1_send("N", 1, 1)
    mlp_out(2, False)
    got("Mba")
    share("M", s.WM, 3, "3")
    mlp_grad(2)
    fold_send("M", s.GM, 2)
    z2_send("N", 1, 1)
    got("Md3")
    mlp(3)
    fold("M", s.GM, 2)
    b_send("M", b, 0)
    z1_send("N", 2, 2)
    mlp_out(3, False)
    z_finish("N", 0, 0)
    sent("Md3")
    mlp_grad(3)
    fold_send("M", s.WM, 3)
    spread_sent("cot")
    s.HD[:d] = s.FIN[...].astype(BF16)
    norm_back(1, 0, length)
    fold("M", s.WM, 3)
    b_send("M", 3, 1)
    z1_send("N", 3, 3)
    gather_sent("A", "0")
    gather_sent("A", "a")
    sent("Ad0", "Ada", "Adb", "Ad3", "Aa", "Ab0", "Aba")
    z2_send("N", 2, 2)
    attend_back(3, True, None)
    z_finish("N", 1, 1)
    for k in (1, 2, 3):
        send(f"out{k}", s.HD.at[pl.ds(pl.multiple_of(row[k] * wide, wide), wide)], s.out.at[r], f"r{k}")
    local("out0", s.HD.at[pl.ds(pl.multiple_of(r * wide, wide), wide)], s.out.at[r])
    attend_grad(3)
    fold_send("A", s.WA, 3)
    z2_send("N", 3, 3)
    b_fold("M", 0, 0)
    z1_send("M", 0, 0)
    b_fold("M", a, 1)
    z1_send("M", a, 1)
    fold("A", s.WA, 3)
    b_send("A", 3, 1)
    attend_back(1, False, None)
    z_finish("N", 2, 2)
    attend_grad(1)
    fold_send("A", s.WA, 1)
    z_finish("N", 3, 3)
    b_send("N", b, 0)
    b_send("N", 3, 1)
    z2_send("M", 0, 0)
    attend_back(2, False, None)
    z2_send("M", a, 1)
    fold("A", s.WA, 1)
    attend_grad(2)
    fold_send("A", s.WA, 2)
    fold("A", s.WA, 2)
    b_send("A", b, 0)
    b_fold("A", a, 1)
    z1_send("A", a, 1)
    attend_back(0, False, 0)
    b_fold("N", a, 1)
    z_finish("M", a, 1)
    send("Me", s.GM.at[a, cc, h], s.REM, "a")
    norm_back(0, length // 2, length)

    def dx(k, part):
        at, sl = r if k == 0 else row[k], halves()[part]
        return s.HD.at[pl.ds(pl.multiple_of(d + at * wide, wide), wide), sl], s.dx.at[r, :, sl]

    for k in (1, 2, 3):
        send(f"dx{k}_1", *dx(k, 1), f"r{k}")
    local("dx0_1", *dx(0, 1))
    z2_send("A", a, 1)
    attend_back(0, False, 1)
    attend_grad(0)
    fold_send("A", s.WA, 0)
    norm_back(0, 0, length // 2)
    for k in (1, 2, 3):
        send(f"gz{k}", s.GG, s.RZ.at[k - 1], f"z{k}")
    b_fold("A", 0, 0)
    fold("A", s.WA, 0)
    z1_send("A", 0, 0)
    got("gz1", "gz2", "gz3")
    s.GS[0] = (s.GG[...] + s.RZ[0]) + (s.RZ[1] + s.RZ[2])
    send("gd", s.GS.at[0], s.RZ.at[3], "dp")
    z_finish("A", a, 1)
    send("Ae", s.WA.at[a, cc, h], s.REA, "a")
    got("gd")
    s.GS[1] = s.GS[0] + s.RZ[3]
    for k in (1, 2, 3):
        send(f"gg{k}", s.GS.at[1, row[k]], s.RG.at[k - 1], f"r{k}")
    for k in (1, 2, 3):
        send(f"dx{k}_0", *dx(k, 0), f"r{k}")
    local("dx0_0", *dx(0, 0))
    z2_send("A", 0, 0)
    z_finish("M", 0, 0)
    b_fold("N", 0, 0)
    got("Me")
    add(s.GM.at[0, cc, h], s.REM)
    send("Mf", s.GM.at[0, cc, h], s.grads.at[h, :, la:], "dp")
    local("Mf0", s.GM.at[0, cc, h], s.grads.at[h, :, la:])
    got("gg1", "gg2", "gg3")
    s.RG[3] = (s.GS[1, r] + s.RG[0]) + (s.RG[1] + s.RG[2])
    local("gg", s.RG.at[3], s.gain_grads)
    z_finish("A", 0, 0)
    got("Ae")
    add(s.WA.at[0, cc, h], s.REA)
    send("Af", s.WA.at[0, cc, h], s.grads.at[h, :, :la], "dp")
    local("Af0", s.WA.at[0, cc, h], s.grads.at[h, :, :la])
    done("gg", "Mf0", "Af0", "out0", "dx0_0", "dx0_1")
    got("Mf", "Af")
    for name in ("out{}", "dx{}_0", "dx{}_1"):
        got(*(name.format(k) for k in (1, 2, 3)))
        sent(*(name.format(k) for k in (1, 2, 3)))
    spread_sent("hid")
    spread_sent("gain")
    sent("Ma", "Me", "Mf", "Ae", "Af", "gd", *(f"{name}{k}" for name in ("gg", "gz") for k in (1, 2, 3)))
    gather_sent("M", "0")
    gather_sent("M", "a")
    sent("Md0", "Mda", "Mdb", "Mdb'", "Mb0", "Mb0'", "Mba")
    for tag, count in (("A", 2), ("M", 2), ("N", 4)):
        sent(*(f"{tag}_half{k}" for k in (0, 1)))
        sent(*(f"{tag}_{kind}{k}" for kind in ("far", "near", "last") for k in range(count)))
    sent(*(f"{tag}_fold{i}" for tag in "AM" for i in range(4)))


class Refs:
    def __init__(self, names, refs):
        self.__dict__.update(zip(names, refs, strict=True))


INPUTS = ("lengths", "hidden", "cot", "w", "gains", "cos", "sin")
OUTPUTS = ("out", "dx", "grads", "gain_grads")


def shards(groups, hidden, lengths, w_qkv, w_out, w_gate_up, w_down, gain_attn, gain_mlp, cotangent):
    _, wide, length = hidden.shape
    d, ff = 4 * wide, w_gate_up.shape[2]
    rows = w_qkv.shape[0]
    w, gains = prepare(w_out, w_qkv.transpose(1, 0, 2), w_gate_up, w_down.T, gain_attn, gain_mlp)
    cols = lax.axis_size("col")
    clubs = [[g * groups + i for i in range(groups)] for g in range(cols // groups)]
    if groups > 1:
        w = lax.all_gather(w, "col", axis_index_groups=clubs, axis=0, tiled=True)
    la, lm, eighth = 4 * wide, 3 * ff, d // 8
    freq = np.exp(np.arange(E // 2, dtype=np.float32) * np.float32(-2.0 * math.log(10000.0) / E))
    angles = freq[:, None] * np.arange(length, dtype=np.float32)[None, :]
    heads = d // E
    scratch = {
        "WA": pltpu.VMEM((4, 4, 2, eighth, la), BF16),
        "WM": pltpu.VMEM((4, 4, 2, eighth, lm), BF16),
        "GM": pltpu.VMEM((3, 4, 2, eighth, lm), BF16),
        "X": pltpu.VMEM((4, wide, length), BF16),
        "G": pltpu.VMEM((4, wide, length), BF16),
        "GAIN": pltpu.VMEM((4, 16, 256), BF16),
        "GC": pltpu.VMEM((d, 128), F32),
        "N1": pltpu.VMEM((d, length), BF16),
        "N2": pltpu.VMEM((d, length), BF16),
        "Q": pltpu.VMEM((heads, E + 16, length), BF16),
        "K": pltpu.VMEM((heads, E + 16, length), BF16),
        "V": pltpu.VMEM((heads, E + 16, length), BF16),
        "ATT": pltpu.VMEM((4, 256, length), BF16),
        "MID": pltpu.VMEM((d, length), F32),
        "FIN": pltpu.VMEM((d, length), F32),
        "DN": pltpu.VMEM((d, length), F32),
        "HD": pltpu.VMEM((3 * ff, length), BF16),
        "R": pltpu.VMEM((8, length), F32),
        "GG": pltpu.VMEM((4, 8, 256), F32),
        "RG": pltpu.VMEM((4, 8, 256), F32),
        "GS": pltpu.VMEM((2, 4, 8, 256), F32),
        "RZ": pltpu.VMEM((4, 4, 8, 256), F32),
        "RDM": pltpu.VMEM((4, 4, eighth, lm), BF16),
        "RBA": pltpu.VMEM((2, 4, eighth, la), BF16),
        "RBM": pltpu.VMEM((2, 4, eighth, lm // 2), BF16),
        "RBN": pltpu.VMEM((2, eighth, lm // 2), BF16),
        "RZA": pltpu.VMEM((2, 2, eighth, la), BF16),
        "RZM": pltpu.VMEM((2, 2, eighth, lm // 2), BF16),
        "RZN": pltpu.VMEM((4, 2, eighth, lm // 2), BF16),
        "RYA": pltpu.VMEM((2, eighth, la), BF16),
        "RYM": pltpu.VMEM((2, eighth, lm // 2), BF16),
        "RYN": pltpu.VMEM((4, eighth, lm // 2), BF16),
        "REA": pltpu.VMEM((eighth, la), BF16),
        "REM": pltpu.VMEM((eighth, lm), BF16),
        "ssem": pltpu.SemaphoreType.DMA((N_COPIES,)),
        "rsem": pltpu.SemaphoreType.DMA((N_COPIES,)),
    }

    def kernel(*refs):
        layer(groups, Refs((*INPUTS, *OUTPUTS, *scratch), refs))

    anywhere, vmem = pl.BlockSpec(memory_space=pl.ANY), pl.BlockSpec(memory_space=pltpu.VMEM)
    out, dx, grad, gain_grads = pl.pallas_call(
        kernel,
        out_shape=(
            jax.ShapeDtypeStruct(hidden.shape, BF16),
            jax.ShapeDtypeStruct(hidden.shape, BF16),
            jax.ShapeDtypeStruct((2, eighth, la + lm), BF16),
            jax.ShapeDtypeStruct((8, 256), F32),
        ),
        in_specs=[pl.BlockSpec(memory_space=pltpu.SMEM), *[anywhere] * 4, vmem, vmem],
        out_specs=(anywhere,) * 4,
        scratch_shapes=list(scratch.values()),
        compiler_params=pltpu.CompilerParams(
            collective_id=0, has_side_effects=True, vmem_limit_bytes=63 * 2**20
        ),
    )(lengths, hidden, cotangent, w.reshape(2, eighth, la + lm), gains, np.cos(angles), np.sin(angles))
    grad = grad.reshape(d // 4, la + lm)
    if groups > 1:
        grad = lax.psum_scatter(grad, "col", axis_index_groups=clubs, scatter_dimension=0, tiled=True)
        gain_grads = lax.psum(gain_grads, "col", axis_index_groups=clubs)
    out, dx, g_qkv, g_out, g_gu, g_down, g_one, g_two = finish(out, dx, grad, gain_grads, wide, ff)
    return (out, dx, g_qkv.transpose(1, 0, 2), g_out, g_gu, g_down.T, g_one, g_two)


def prepare(w_out, w_qkv, w_gate_up, w_down, gain_attn, gain_mlp):
    _, rows, wide = w_qkv.shape
    ff = w_down.shape[1]

    def kernel(out_ref, qkv_ref, gu_ref, down_ref, one_ref, two_ref, w_ref, gain_ref):
        w_ref[:, :wide] = out_ref[...].astype(F32).T.astype(BF16)
        for k in range(3):
            w_ref[:, (k + 1) * wide : (k + 2) * wide] = qkv_ref[k]
        for k in range(2):
            w_ref[:, 4 * wide + k * ff : 4 * wide + (k + 1) * ff] = gu_ref[:, k, :]
        w_ref[:, 4 * wide + 2 * ff :] = down_ref[...]
        one, two = (jnp.broadcast_to(v[...].astype(F32).reshape(1, wide), (16, wide)) for v in (one_ref, two_ref))
        row = lax.broadcasted_iota(jnp.int32, (16, wide), 0)
        gain_ref[...] = jnp.zeros(gain_ref.shape, BF16)
        gain_ref[:, :wide] = jnp.where(row == 0, one, two).astype(BF16)

    return pl.pallas_call(
        kernel,
        out_shape=(
            jax.ShapeDtypeStruct((rows, 4 * wide + 3 * ff), BF16),
            jax.ShapeDtypeStruct((16, 256), BF16),
        ),
    )(w_out, w_qkv, w_gate_up, w_down, gain_attn, gain_mlp)


def finish(out, dx, grad, gain_grads, wide, ff):
    n, _, length = out.shape
    rows = grad.shape[0]

    def kernel(out_in, dx_in, grad_in, gain_in, out_ref, dx_ref, qkv_ref, back_ref, gu_ref, down_ref, one_ref, two_ref):
        out_ref[...] = out_in[...]
        dx_ref[...] = dx_in[...].astype(F32)

        @pl.when(pl.program_id(0) == 0)
        def _():
            g = grad_in[...].astype(F32)
            back_ref[...] = g[:, :wide].T
            for k in range(3):
                qkv_ref[k] = g[:, (k + 1) * wide : (k + 2) * wide]
            for k in range(2):
                gu_ref[:, k, :] = g[:, 4 * wide + k * ff : 4 * wide + (k + 1) * ff]
            down_ref[...] = g[:, 4 * wide + 2 * ff :]
            one_ref[...] = gain_in[0, :wide]
            two_ref[...] = gain_in[1, :wide]

    def block(*shape):
        return pl.BlockSpec(shape, lambda i: (0,) * len(shape))

    tokens = pl.BlockSpec((1, wide, length), lambda i: (i, 0, 0))
    shapes = ((3, rows, wide), (wide, rows), (rows, 2, ff), (rows, ff), (wide,), (wide,))
    return pl.pallas_call(
        kernel,
        grid=(n,),
        out_shape=(
            jax.ShapeDtypeStruct(out.shape, BF16),
            jax.ShapeDtypeStruct(out.shape, F32),
            *(jax.ShapeDtypeStruct(shape, F32) for shape in shapes),
        ),
        in_specs=[tokens, tokens, block(*grad.shape), block(*gain_grads.shape)],
        out_specs=(tokens, tokens, *(block(*shape) for shape in shapes)),
        compiler_params=pltpu.CompilerParams(vmem_limit_bytes=60 * 2**20),
    )(out, dx, grad, gain_grads)


def solution(mesh):
    tokens, wide = P(("dp", "col"), "row", None), P("col", None, "row")
    back, gain = P("row", "col"), P("row")
    return jax.shard_map(
        functools.partial(shards, mesh.shape["col"] // 4),
        mesh=mesh,
        in_specs=(tokens, P(("dp", "col")), wide, back, wide, back, gain, gain, tokens),
        out_specs=(tokens, tokens, wide, back, wide, back, gain, gain),
        check_vma=False,
    )
```

```python
import functools
import math

import jax
import jax.numpy as jnp
import numpy as np
from jax import lax
from jax.experimental import pallas as pl
from jax.experimental.pallas import tpu as pltpu
from jax.sharding import PartitionSpec as P

EPS = 1e-05
E = 64
C = 256
LOG2E = math.log2(math.e)
F32, BF16 = jnp.float32, jnp.bfloat16
N_COPIES = 128


def dg(a, b, contract):
    return lax.dot_general(a, b, ((contract[:1], contract[1:]), ((), ())), preferred_element_type=F32)


def rope(v, cos, sin, sign):
    half = v.shape[0] // 2
    a, b = v[:half], v[half:]
    return jnp.concatenate([a * cos - sign * (b * sin), b * cos + sign * (a * sin)], axis=0)


def pack_rows(values, width):
    row = lax.broadcasted_iota(jnp.int32, (16, width), 0)
    out = jnp.zeros((16, width), F32)
    for i, v in enumerate(values):
        out = jnp.where(row == i, v, out)
    return out.astype(BF16)


def split3(v):
    hi = v.astype(BF16).astype(F32)
    mid = (v - hi).astype(BF16).astype(F32)
    return hi, mid, v - hi - mid


def layer(groups, refs):
    s = refs
    d, length = s.N1.shape
    wide = s.X.shape[1]
    heads = wide // E
    ff = s.HD.shape[0] // 3
    la, lm = 4 * wide, 3 * ff
    n_blk = length // C

    h, r, c = lax.axis_index("dp"), lax.axis_index("row"), lax.axis_index("col")
    cc, ci = c // groups, c % groups
    col = {1: cc + 1 - 2 * (cc % 2), 2: (cc + 2) % 4, 3: 3 - cc}
    row = {1: r + 1 - 2 * (r % 2), 2: (r + 2) % 4, 3: 3 - r}
    a, b = 1 + h, 2 - h
    to = {
        "dp": {"dp": 1 - h},
        "z1": {"col": col[1] * groups + ci},
        "z2": {"col": col[2] * groups + ci},
        "r1": {"row": row[1]},
        "r2": {"row": row[2]},
        "r3": {"row": row[3]},
        "z3": {"col": col[3] * groups + ci},
        "a": {"row": (1 - h) * row[1] + h * row[2]},
        "b": {"row": (1 - h) * row[2] + h * row[1]},
    }
    copies = {}
    parts = {"A": (0, la), "M": (la, la + lm)}

    def send(name, src, dst, where):
        assert name not in copies, name
        n = len(copies)
        copies[name] = pltpu.make_async_remote_copy(
            src_ref=src,
            dst_ref=dst,
            send_sem=s.ssem.at[n],
            recv_sem=s.rsem.at[n],
            device_id=to[where],
            device_id_type=pl.DeviceIdType.MESH,
        )
        copies[name].start()

    def local(name, src, dst):
        assert name not in copies, name
        n = len(copies)
        copies[name] = pltpu.make_async_copy(src, dst, s.ssem.at[n])
        copies[name].start()

    def got(*names):
        for name in names:
            copies[name].wait_recv()

    def sent(*names):
        for name in names:
            copies[name].wait_send()

    def done(*names):
        for name in names:
            copies[name].wait()

    def add(dst, src):
        dst[...] = (dst[...].astype(F32) + src[...].astype(F32)).astype(BF16)

    def phase(body):
        def run(*args):
            pl.when(r < 4)(functools.partial(body, *args))

        return run

    def w_a(i, lo=0, hi=la):
        return s.WA[i, :, :, :, lo:hi].reshape(d, hi - lo)

    def w_m(i, lo=0, hi=3 * ff):
        return s.WM[i, :, :, :, lo:hi].reshape(d, hi - lo)

    def put(ref, i, lo, value):
        n = value.shape[1]
        ref[i, :, :, :, lo : lo + n] = value.astype(BF16).reshape(4, 2, d // 8, n)

    def grad_m(i):
        return s.WM if isinstance(i, int) and i == 3 else s.GM

    def blocks():
        return [slice(j * C, (j + 1) * C) for j in range(n_blk)]

    def gain(which):
        return s.GC[:, which : which + 1]

    @phase
    def gain_columns():
        for k in range(4):
            turned = jnp.concatenate([s.GAIN[k].astype(F32)] * 8, axis=0).T
            s.GC[k * wide : (k + 1) * wide] = turned[:wide]

    def x_of(sl):
        return s.X[:, :, sl].reshape(d, sl.stop - sl.start).astype(F32)

    @phase
    def setup():
        s.ATT[:, wide:] = jnp.zeros((4, s.ATT.shape[1] - wide, length), BF16)
        s.GG[...] = jnp.zeros(s.GG.shape, F32)
        pos = lax.broadcasted_iota(jnp.int32, (1, length), 1)
        bias = jnp.where(pos < s.lengths[r], 0.0, -1e30)
        shape = (4 * heads, 16, length)
        s.K[:, E:] = jnp.broadcast_to(pack_rows([bias, 1.0, 1.0, 1.0], length), shape)
        s.Q[:, E:] = jnp.broadcast_to(pack_rows([1.0], length), shape)
        s.V[:, E:] = jnp.broadcast_to(pack_rows([1.0, 1.0, 1.0], length), shape)

    @phase
    def norm(which):
        for sl in blocks():
            x = s.MID[:, sl] if which else x_of(sl)
            inv = lax.rsqrt(jnp.sum(x * x, axis=0, keepdims=True) * (1.0 / d) + EPS)
            s.R[which : which + 1, sl] = inv
            (s.N2 if which else s.N1)[:, sl] = (x * inv * gain(which)).astype(BF16)

    def halves():
        return [slice(0, length // 2), slice(length // 2, length)]

    @phase
    def project(i):
        for sl in halves():
            p = dg(w_a(i), s.N1[:, sl], (0, 0))
            cos, sin = s.cos[:, sl], s.sin[:, sl]
            for k in range(heads):
                part = [p[n * wide + k * E : n * wide + (k + 1) * E] for n in (1, 2, 3)]
                s.Q[heads * i + k, :E, sl] = (rope(part[0], cos, sin, 1.0) * (LOG2E / math.sqrt(E))).astype(BF16)
                s.K[heads * i + k, :E, sl] = rope(part[1], cos, sin, 1.0).astype(BF16)
                s.V[heads * i + k, :E, sl] = part[2].astype(BF16)

    def causal():
        return lax.broadcasted_iota(jnp.int32, (C, C), 0) <= lax.broadcasted_iota(jnp.int32, (C, C), 1)

    @phase
    def attend(i):
        tri = causal()
        items = [(k, j) for k in range(heads) for j in range(n_blk)]
        lse = []

        def scores(k, j):
            return dg(s.K[heads * i + k, :, : (j + 1) * C], s.Q[heads * i + k, :, j * C : (j + 1) * C], (0, 0))

        def soft(v, j):
            n = j * C
            diag = jnp.where(tri, v[n:], -1e30)
            top = jnp.max(diag, axis=0, keepdims=True)
            if j:
                top = jnp.maximum(top, jnp.max(v[:n], axis=0, keepdims=True))
            e = jnp.exp2(diag - top).astype(BF16)
            if j:
                e = jnp.concatenate([jnp.exp2(v[:n] - top).astype(BF16), e], axis=0)
            return top, e

        def mix(k, j, top, e):
            sl = slice(j * C, (j + 1) * C)
            o = dg(s.V[heads * i + k, :, : (j + 1) * C], e, (1, 0))
            total = o[E : E + 1]
            s.ATT[i, k * E : (k + 1) * E, sl] = (o[:E] * (1.0 / total)).astype(BF16)
            lse.append((k, sl, pack_rows([1.0, *split3(-(top + jnp.log2(total)))], C)))

        held, now = None, scores(*items[0])
        for n, (k, j) in enumerate(items):
            later = scores(*items[n + 1]) if n + 1 < len(items) else None
            top, e = soft(now, j)
            if held:
                mix(*held)
            held, now = (k, j, top, e), later
        mix(*held)
        for k, sl, rows in lse:
            s.Q[heads * i + k, E:, sl] = rows

    @phase
    def out_project():
        for i in range(4):
            for sl in halves():
                y = dg(w_a(i, 0, s.ATT.shape[1]), s.ATT[i, :, sl], (1, 0))
                s.MID[:, sl] = (s.MID[:, sl] if i else s.X[:, :, sl].reshape(d, length // 2).astype(F32)) + y

    @phase
    def mlp(i):

        def dots(sl):
            gu = dg(w_m(i, 0, 2 * ff), s.N2[:, sl], (0, 0))
            return gu, dg(w_m(i, 2 * ff), s.G[:, :, sl].reshape(d, C), (0, 0))

        def mix(sl, gu, d_hid):
            gate, up = gu[:ff], gu[ff:]
            sig = 1.0 / (1.0 + jnp.exp(-gate))
            silu = gate * sig
            s.HD[:ff, sl] = (silu * up).astype(BF16)
            s.HD[ff : 2 * ff, sl] = (d_hid * up * (sig + silu * (1.0 - sig))).astype(BF16)
            s.HD[2 * ff :, sl] = (d_hid * silu).astype(BF16)

        now = dots(blocks()[0])
        for j, sl in enumerate(blocks()):
            later = dots(blocks()[j + 1]) if j + 1 < n_blk else None
            mix(sl, *now)
            now = later

    @phase
    def mlp_out(i, first):
        for sl in halves():
            y = dg(w_m(i, 2 * ff), s.HD[:ff, sl], (1, 0))
            s.FIN[:, sl] = (s.MID if first else s.FIN)[:, sl] + y
            z = dg(w_m(i, 0, 2 * ff), s.HD[ff:, sl], (1, 0))
            s.DN[:, sl] = z if first else s.DN[:, sl] + z

    @phase
    def mlp_grad(i):
        put(grad_m(i), i, 0, dg(s.N2[...], s.HD[ff : 2 * ff], (1, 1)))
        put(grad_m(i), i, ff, dg(s.N2[...], s.HD[2 * ff :], (1, 1)))
        put(grad_m(i), i, 2 * ff, dg(s.G[...].reshape(d, length), s.HD[:ff], (1, 1)))

    @phase
    def norm_back(which, lo, hi):
        total = jnp.zeros((d, 128), F32)
        for j in range(lo, hi, 128):
            sl = slice(j, j + 128)
            dn = (s.DN if which else s.FIN)[:, sl]
            inv = s.R[which : which + 1, sl]
            unit = (s.MID[:, sl] if which else x_of(sl)) * inv
            e = dn * gain(which)
            inner = jnp.sum(e * unit, axis=0, keepdims=True) * (1.0 / d)
            dv = inv * (e - unit * inner)
            total = total + dn * unit
            if which:
                dm = s.G[:, :, sl].reshape(d, 128).astype(F32) + dv
                s.DN[:, sl] = dm
                s.N2[:, sl] = dm.astype(BF16)
            else:
                s.HD[d:, sl] = (s.DN[:, sl] + dv).astype(BF16)
        line = jnp.sum(total.T, axis=0, keepdims=True)
        for k in range(4):
            s.GG[k, which : which + 1, :wide] += line[:, k * wide : (k + 1) * wide]

    dr = E + 16

    @phase
    def attend_back(i, first, part):
        if part != 1:
            d_o = dg(w_a(i, 0, s.ATT.shape[1]), s.N2[...], (0, 0))[:wide].astype(BF16)
            for k in range(heads):
                mine = d_o[k * E : (k + 1) * E]
                s.HD[d + k * dr : d + k * dr + E] = mine
                inner = jnp.sum(mine.astype(F32) * s.ATT[i, k * E : (k + 1) * E].astype(F32), axis=0, keepdims=True)
                s.HD[d + k * dr + E : d + (k + 1) * dr] = pack_rows(split3(-inner), length)
        tri = causal()
        mid = n_blk // 2 if part == 0 else 0
        items = [(k, j) for k in range(heads) for j in range(mid, n_blk if part != 1 else n_blk // 2)]

        def start(k, j):
            n, sl, g = (j + 1) * C, slice(j * C, (j + 1) * C), heads * i + k
            return dg(s.K[g, :, :n], s.Q[g, :, sl], (0, 0)), dg(
                s.V[g, :, :n], s.HD[d + k * dr : d + (k + 1) * dr, sl], (0, 0)
            )

        def finish(k, j, sc, dp):
            n, sl, g = (j + 1) * C, slice(j * C, (j + 1) * C), heads * i + k
            p = jnp.where(tri, jnp.exp2(sc[n - C :]), 0.0)
            if j:
                p = jnp.concatenate([jnp.exp2(sc[: n - C]), p], axis=0)
            ds, p = (p * dp).astype(BF16), p.astype(BF16)
            s.MID[k * E : (k + 1) * E, sl] = dg(s.K[g, :E, :n], ds, (1, 0))
            dk, dv = dg(s.Q[g, :E, sl], ds, (1, 1)), dg(s.HD[d + k * dr : d + k * dr + E, sl], p, (1, 1))
            at = slice(wide + k * E, wide + (k + 1) * E), slice(2 * wide + k * E, 2 * wide + (k + 1) * E)
            if part != 1 and j == mid:
                s.MID[at[0], n:] = jnp.zeros((E, length - n), F32)
                s.MID[at[1], n:] = jnp.zeros((E, length - n), F32)
                s.MID[at[0], :n] = dk
                s.MID[at[1], :n] = dv
            else:
                s.MID[at[0], :n] += dk
                s.MID[at[1], :n] += dv

        now = start(*items[0])
        for n, (k, j) in enumerate(items):
            later = start(*items[n + 1]) if n + 1 < len(items) else None
            finish(k, j, *now)
            now = later
        for sl in halves() if part is None else halves()[1 - part : 2 - part]:
            cos, sin = s.cos[:, sl], s.sin[:, sl]
            dp = [jnp.zeros((wide, length // 2), BF16)]
            for n, scale in enumerate((1.0 / math.sqrt(E), 1.0 / LOG2E, None)):
                for k in range(heads):
                    v = s.MID[n * wide + k * E : n * wide + (k + 1) * E, sl]
                    dp.append((v if scale is None else rope(v * scale, cos, sin, -1.0)).astype(BF16))
            dp = jnp.concatenate(dp, axis=0)
            s.RDM[:2, :, :, sl] = dp.reshape(2, 4, d // 8, length // 2)
            z = dg(w_a(i), dp, (1, 0))
            s.FIN[:, sl] = z if first else s.FIN[:, sl] + z

    @phase
    def attend_grad(i):
        dp = s.RDM[:2, :, :, :length].reshape(d, length)
        gq, go = dg(s.N1[...], dp, (1, 1)), dg(s.N2[...], s.ATT[i], (1, 1))
        n = go.shape[1]
        put(s.WA, i, 0, gq[:, :n] + go)
        put(s.WA, i, n, gq[:, n:])

    def own(ref, lo, hi):
        return ref.at[h, :, lo:hi]

    def spread(name, src, dst):
        for k in (1, 2, 3):
            send(f"{name}{k}", src(row[k]), dst(r), f"r{k}")
        local(f"{name}0", src(r), dst(r))

    def spread_got(name):
        got(*(f"{name}{k}" for k in (1, 2, 3)))
        done(f"{name}0")

    def spread_sent(name):
        sent(*(f"{name}{k}" for k in (1, 2, 3)))

    def piece(tag, slot, at):
        lo, hi = parts[tag]
        if lo < la:
            return s.WA.at[slot, at, h, :, lo:hi]
        return s.WM.at[slot, at, h, :, lo - la : hi - la]

    def gather_z(tag, slot, name, source=None):
        src, dst = source or piece(tag, slot, cc), piece(tag, slot, cc)
        send(f"{tag}z2_{name}", src, dst, "z2")
        send(f"{tag}z1_{name}", src, dst, "z1")

    def gather_z1(tag, slot, name):
        got(f"{tag}z2_{name}")
        send(f"{tag}z12_{name}", piece(tag, slot, col[2]), piece(tag, slot, col[2]), "z1")

    def gathered(tag, name):
        got(f"{tag}z1_{name}", f"{tag}z12_{name}")

    def gather_sent(tag, name):
        sent(*(f"{tag}z{k}_{name}" for k in ("1", "2", "12")))

    def share(tag, ref, slot, name, at=slice(None)):
        send(f"{tag}d{name}", ref.at[slot, at, h], ref.at[slot, at, h], "dp")

    def landing(tag, i):
        if tag == "M":
            return s.RDM.at[i]
        n = (3, 1, 2, 0).index(i)
        return s.RDM.at[2 + n // 2, :, :, n % 2 * la : (n % 2 + 1) * la]

    def fold(tag, ref, i):
        got(f"{tag}_fold{i}")
        add(ref.at[i, :, h], landing(tag, i))

    def fold_send(tag, ref, i):
        send(f"{tag}_fold{i}", ref.at[i, :, 1 - h], landing(tag, i), "dp")

    ways = {
        "A": (s.WA, s.RBA, s.RZA, s.RYA, 0, la),
        "M": (s.GM, s.RBM, s.RZM, s.RYM, 0, lm // 2),
        "N": (s.GM, s.RBN, s.RZN, s.RYN, lm // 2, lm),
    }

    def spot(tag, slot, at):
        ref, _, _, _, lo, hi = ways[tag]
        if tag != "A":
            ref = grad_m(slot)
        return ref.at[slot, at, h, :, lo:hi]

    def b_send(tag, slot, k):
        at = cc if tag == "N" else slice(None)
        send(f"{tag}_half{k}", spot(tag, slot, at), ways[tag][1].at[k], "b")

    def b_fold(tag, slot, k):
        got(f"{tag}_half{k}")
        add(spot(tag, slot, cc if tag == "N" else slice(None)), ways[tag][1].at[k])

    def z1_send(tag, slot, k):
        send(f"{tag}_far{k}", spot(tag, slot, col[3]), ways[tag][2].at[k, 1], "z1")

    def z2_send(tag, slot, k):
        got(f"{tag}_far{k}")
        add(spot(tag, slot, col[2]), ways[tag][2].at[k, 1])
        send(f"{tag}_last{k}", spot(tag, slot, col[2]), ways[tag][3].at[k], "z2")
        send(f"{tag}_near{k}", spot(tag, slot, col[1]), ways[tag][2].at[k, 0], "z1")

    def z_finish(tag, slot, k):
        got(f"{tag}_near{k}", f"{tag}_last{k}")
        mine = spot(tag, slot, cc)
        mine[...] = (
            mine[...].astype(F32) + ways[tag][2][k, 0].astype(F32) + ways[tag][3][k].astype(F32)
        ).astype(BF16)

    barrier = pltpu.get_barrier_semaphore()
    friends = ("dp", "z1", "z2", "z3", "r1", "r2", "r3")
    for name in friends:
        pl.semaphore_signal(barrier, inc=1, device_id=to[name], device_id_type=pl.DeviceIdType.MESH)
    pl.semaphore_wait(barrier, len(friends))

    both = (("", slice(0, 2)), ("'", slice(2, 4)))
    send("Aa", own(s.w, *parts["A"]), piece("A", a, cc), "a")
    gather_z("A", 0, "0", own(s.w, *parts["A"]))
    send("Ma", own(s.w, *parts["M"]), piece("M", a, cc), "a")
    spread("hid", lambda i: s.hidden.at[i], lambda i: s.X.at[i])
    spread("gain", lambda i: s.gains, lambda i: s.GAIN.at[i])
    local("A0", own(s.w, 0, la), s.WA.at[0, cc, h])
    local("M0", own(s.w, la, la + lm), s.WM.at[0, cc, h])
    setup()
    got("Aa")
    gather_z("A", a, "a")
    gather_z1("A", 0, "0")
    gather_z1("A", a, "a")
    gathered("A", "0")
    done("A0", "M0")
    share("A", s.WA, 0, "0")
    send("Ab0", piece("A", 0, slice(None)), piece("A", b, slice(None)), "b")
    gathered("A", "a")
    share("A", s.WA, a, "a")
    send("Aba", piece("A", a, slice(None)), piece("A", 3, slice(None)), "b")
    gather_z("M", 0, "0")
    spread_got("hid")
    spread("cot", lambda i: s.cot.at[i], lambda i: s.G.at[i])
    spread_got("gain")
    gain_columns()
    norm(0)
    got("Ad0")
    project(0)
    attend(0)
    gather_z1("M", 0, "0")
    got("Ma")
    gather_z("M", a, "a")
    got("Ab0")
    share("A", s.WA, b, "b")
    got("Ada", "Adb")
    project(1)
    attend(1)
    project(2)
    got("Aba")
    share("A", s.WA, 3, "3")
    attend(2)
    got("Ad3")
    project(3)
    attend(3)
    gathered("M", "0")
    share("M", s.WM, 0, "0")
    for tick, at in both:
        send(f"Mb0{tick}", piece("M", 0, at), piece("M", b, at), "b")
    gather_z1("M", a, "a")
    out_project()
    norm(1)
    got("Md0")
    spread_got("cot")
    mlp(0)
    mlp_out(0, True)
    gathered("M", "a")
    share("M", s.WM, a, "a")
    send("Mba", piece("M", a, slice(None)), piece("M", 3, slice(None)), "b")
    mlp_grad(0)
    fold_send("M", s.GM, 0)
    for tick, at in both:
        got(f"Mb0{tick}")
        share("M", s.WM, b, f"b{tick}", at)
    fold("M", s.GM, 0)
    z1_send("N", 0, 0)
    got("Mda", "Mdb", "Mdb'")
    mlp(1)
    mlp_out(1, False)
    z2_send("N", 0, 0)
    mlp_grad(1)
    fold_send("M", s.GM, 1)
    mlp(2)
    fold("M", s.GM, 1)
    z1_send("N", 1, 1)
    mlp_out(2, False)
    got("Mba")
    share("M", s.WM, 3, "3")
    mlp_grad(2)
    fold_send("M", s.GM, 2)
    z2_send("N", 1, 1)
    got("Md3")
    mlp(3)
    fold("M", s.GM, 2)
    b_send("M", b, 0)
    z1_send("N", 2, 2)
    mlp_out(3, False)
    z_finish("N", 0, 0)
    sent("Md3")
    mlp_grad(3)
    fold_send("M", s.WM, 3)
    spread_sent("cot")
    s.HD[:d] = s.FIN[...].astype(BF16)
    norm_back(1, 0, length)
    fold("M", s.WM, 3)
    b_send("M", 3, 1)
    z1_send("N", 3, 3)
    gather_sent("A", "0")
    gather_sent("A", "a")
    sent("Ad0", "Ada", "Adb", "Ad3", "Aa", "Ab0", "Aba")
    z2_send("N", 2, 2)
    attend_back(3, True, None)
    b_fold("M", 0, 0)
    z1_send("M", 0, 0)
    z_finish("N", 1, 1)
    for k in (1, 2, 3):
        send(f"out{k}", s.HD.at[pl.ds(pl.multiple_of(row[k] * wide, wide), wide)], s.out.at[r], f"r{k}")
    local("out0", s.HD.at[pl.ds(pl.multiple_of(r * wide, wide), wide)], s.out.at[r])
    attend_grad(3)
    fold_send("A", s.WA, 3)
    z2_send("N", 3, 3)
    b_fold("M", a, 1)
    z1_send("M", a, 1)
    fold("A", s.WA, 3)
    b_send("A", 3, 1)
    attend_back(1, False, None)
    z_finish("N", 2, 2)
    attend_grad(1)
    fold_send("A", s.WA, 1)
    z2_send("M", 0, 0)
    z_finish("N", 3, 3)
    b_send("N", b, 0)
    b_send("N", 3, 1)
    attend_back(2, False, None)
    z2_send("M", a, 1)
    fold("A", s.WA, 1)
    attend_grad(2)
    fold_send("A", s.WA, 2)
    fold("A", s.WA, 2)
    b_send("A", b, 0)
    b_fold("A", a, 1)
    z1_send("A", a, 1)
    attend_back(0, False, 0)
    norm_back(0, length // 2, length)

    def dx(k, part):
        at, sl = r if k == 0 else row[k], halves()[part]
        return s.HD.at[pl.ds(pl.multiple_of(d + at * wide, wide), wide), sl], s.dx.at[r, :, sl]

    for k in (1, 2, 3):
        send(f"dx{k}_1", *dx(k, 1), f"r{k}")
    local("dx0_1", *dx(0, 1))
    b_fold("N", a, 1)
    z_finish("M", a, 1)
    send("Me", s.GM.at[a, cc, h], s.REM, "a")
    attend_back(0, False, 1)
    z2_send("A", a, 1)
    attend_grad(0)
    fold_send("A", s.WA, 0)
    norm_back(0, 0, length // 2)
    for k in (1, 2, 3):
        send(f"gz{k}", s.GG, s.RZ.at[k - 1], f"z{k}")
    b_fold("A", 0, 0)
    fold("A", s.WA, 0)
    z1_send("A", 0, 0)
    got("gz1", "gz2", "gz3")
    s.GS[0] = (s.GG[...] + s.RZ[0]) + (s.RZ[1] + s.RZ[2])
    send("gd", s.GS.at[0], s.RZ.at[3], "dp")
    z_finish("A", a, 1)
    send("Ae", s.WA.at[a, cc, h], s.REA, "a")
    got("gd")
    s.GS[1] = s.GS[0] + s.RZ[3]
    for k in (1, 2, 3):
        send(f"gg{k}", s.GS.at[1, row[k]], s.RG.at[k - 1], f"r{k}")
    for k in (1, 2, 3):
        send(f"dx{k}_0", *dx(k, 0), f"r{k}")
    local("dx0_0", *dx(0, 0))
    z2_send("A", 0, 0)
    z_finish("M", 0, 0)
    b_fold("N", 0, 0)
    got("Me")
    add(s.GM.at[0, cc, h], s.REM)
    send("Mf", s.GM.at[0, cc, h], s.grads.at[h, :, la:], "dp")
    local("Mf0", s.GM.at[0, cc, h], s.grads.at[h, :, la:])
    got("gg1", "gg2", "gg3")
    s.RG[3] = (s.GS[1, r] + s.RG[0]) + (s.RG[1] + s.RG[2])
    local("gg", s.RG.at[3], s.gain_grads)
    z_finish("A", 0, 0)
    got("Ae")
    add(s.WA.at[0, cc, h], s.REA)
    send("Af", s.WA.at[0, cc, h], s.grads.at[h, :, :la], "dp")
    local("Af0", s.WA.at[0, cc, h], s.grads.at[h, :, :la])
    done("gg", "Mf0", "Af0", "out0", "dx0_0", "dx0_1")
    got("Mf", "Af")
    for name in ("out{}", "dx{}_0", "dx{}_1"):
        got(*(name.format(k) for k in (1, 2, 3)))
        sent(*(name.format(k) for k in (1, 2, 3)))
    spread_sent("hid")
    spread_sent("gain")
    sent("Ma", "Me", "Mf", "Ae", "Af", "gd", *(f"{name}{k}" for name in ("gg", "gz") for k in (1, 2, 3)))
    gather_sent("M", "0")
    gather_sent("M", "a")
    sent("Md0", "Mda", "Mdb", "Mdb'", "Mb0", "Mb0'", "Mba")
    for tag, count in (("A", 2), ("M", 2), ("N", 4)):
        sent(*(f"{tag}_half{k}" for k in (0, 1)))
        sent(*(f"{tag}_{kind}{k}" for kind in ("far", "near", "last") for k in range(count)))
    sent(*(f"{tag}_fold{i}" for tag in "AM" for i in range(4)))


class Refs:
    def __init__(self, names, refs):
        self.__dict__.update(zip(names, refs, strict=True))


INPUTS = ("lengths", "hidden", "cot", "w", "gains", "cos", "sin")
OUTPUTS = ("out", "dx", "grads", "gain_grads")


def shards(groups, hidden, lengths, w_qkv, w_out, w_gate_up, w_down, gain_attn, gain_mlp, cotangent):
    _, wide, length = hidden.shape
    d, ff = 4 * wide, w_gate_up.shape[2]
    rows = w_qkv.shape[0]
    w, gains = prepare(w_out, w_qkv.transpose(1, 0, 2), w_gate_up, w_down.T, gain_attn, gain_mlp)
    cols = lax.axis_size("col")
    clubs = [[g * groups + i for i in range(groups)] for g in range(cols // groups)]
    if groups > 1:
        w = lax.all_gather(w, "col", axis_index_groups=clubs, axis=0, tiled=True)
    la, lm, eighth = 4 * wide, 3 * ff, d // 8
    freq = np.exp(np.arange(E // 2, dtype=np.float32) * np.float32(-2.0 * math.log(10000.0) / E))
    angles = freq[:, None] * np.arange(length, dtype=np.float32)[None, :]
    heads = d // E
    scratch = {
        "WA": pltpu.VMEM((4, 4, 2, eighth, la), BF16),
        "WM": pltpu.VMEM((4, 4, 2, eighth, lm), BF16),
        "GM": pltpu.VMEM((3, 4, 2, eighth, lm), BF16),
        "X": pltpu.VMEM((4, wide, length), BF16),
        "G": pltpu.VMEM((4, wide, length), BF16),
        "GAIN": pltpu.VMEM((4, 16, 256), BF16),
        "GC": pltpu.VMEM((d, 128), F32),
        "N1": pltpu.VMEM((d, length), BF16),
        "N2": pltpu.VMEM((d, length), BF16),
        "Q": pltpu.VMEM((heads, E + 16, length), BF16),
        "K": pltpu.VMEM((heads, E + 16, length), BF16),
        "V": pltpu.VMEM((heads, E + 16, length), BF16),
        "ATT": pltpu.VMEM((4, 256, length), BF16),
        "MID": pltpu.VMEM((d, length), F32),
        "FIN": pltpu.VMEM((d, length), F32),
        "DN": pltpu.VMEM((d, length), F32),
        "HD": pltpu.VMEM((3 * ff, length), BF16),
        "R": pltpu.VMEM((8, length), F32),
        "GG": pltpu.VMEM((4, 8, 256), F32),
        "RG": pltpu.VMEM((4, 8, 256), F32),
        "GS": pltpu.VMEM((2, 4, 8, 256), F32),
        "RZ": pltpu.VMEM((4, 4, 8, 256), F32),
        "RDM": pltpu.VMEM((4, 4, eighth, lm), BF16),
        "RBA": pltpu.VMEM((2, 4, eighth, la), BF16),
        "RBM": pltpu.VMEM((2, 4, eighth, lm // 2), BF16),
        "RBN": pltpu.VMEM((2, eighth, lm // 2), BF16),
        "RZA": pltpu.VMEM((2, 2, eighth, la), BF16),
        "RZM": pltpu.VMEM((2, 2, eighth, lm // 2), BF16),
        "RZN": pltpu.VMEM((4, 2, eighth, lm // 2), BF16),
        "RYA": pltpu.VMEM((2, eighth, la), BF16),
        "RYM": pltpu.VMEM((2, eighth, lm // 2), BF16),
        "RYN": pltpu.VMEM((4, eighth, lm // 2), BF16),
        "REA": pltpu.VMEM((eighth, la), BF16),
        "REM": pltpu.VMEM((eighth, lm), BF16),
        "ssem": pltpu.SemaphoreType.DMA((N_COPIES,)),
        "rsem": pltpu.SemaphoreType.DMA((N_COPIES,)),
    }

    def kernel(*refs):
        layer(groups, Refs((*INPUTS, *OUTPUTS, *scratch), refs))

    anywhere, vmem = pl.BlockSpec(memory_space=pl.ANY), pl.BlockSpec(memory_space=pltpu.VMEM)
    out, dx, grad, gain_grads = pl.pallas_call(
        kernel,
        out_shape=(
            jax.ShapeDtypeStruct(hidden.shape, BF16),
            jax.ShapeDtypeStruct(hidden.shape, BF16),
            jax.ShapeDtypeStruct((2, eighth, la + lm), BF16),
            jax.ShapeDtypeStruct((8, 256), F32),
        ),
        in_specs=[pl.BlockSpec(memory_space=pltpu.SMEM), *[anywhere] * 4, vmem, vmem],
        out_specs=(anywhere,) * 4,
        scratch_shapes=list(scratch.values()),
        compiler_params=pltpu.CompilerParams(
            collective_id=0, has_side_effects=True, vmem_limit_bytes=63 * 2**20
        ),
    )(lengths, hidden, cotangent, w.reshape(2, eighth, la + lm), gains, np.cos(angles), np.sin(angles))
    grad = grad.reshape(d // 4, la + lm)
    if groups > 1:
        grad = lax.psum_scatter(grad, "col", axis_index_groups=clubs, scatter_dimension=0, tiled=True)
        gain_grads = lax.psum(gain_grads, "col", axis_index_groups=clubs)
    out, dx, g_qkv, g_out, g_gu, g_down, g_one, g_two = finish(out, dx, grad, gain_grads, wide, ff)
    return (out, dx, g_qkv.transpose(1, 0, 2), g_out, g_gu, g_down.T, g_one, g_two)


def prepare(w_out, w_qkv, w_gate_up, w_down, gain_attn, gain_mlp):
    _, rows, wide = w_qkv.shape
    ff = w_down.shape[1]

    def kernel(out_ref, qkv_ref, gu_ref, down_ref, one_ref, two_ref, w_ref, gain_ref):
        w_ref[:, :wide] = out_ref[...].astype(F32).T.astype(BF16)
        for k in range(3):
            w_ref[:, (k + 1) * wide : (k + 2) * wide] = qkv_ref[k]
        for k in range(2):
            w_ref[:, 4 * wide + k * ff : 4 * wide + (k + 1) * ff] = gu_ref[:, k, :]
        w_ref[:, 4 * wide + 2 * ff :] = down_ref[...]
        one, two = (jnp.broadcast_to(v[...].astype(F32).reshape(1, wide), (16, wide)) for v in (one_ref, two_ref))
        row = lax.broadcasted_iota(jnp.int32, (16, wide), 0)
        gain_ref[...] = jnp.zeros(gain_ref.shape, BF16)
        gain_ref[:, :wide] = jnp.where(row == 0, one, two).astype(BF16)

    return pl.pallas_call(
        kernel,
        out_shape=(
            jax.ShapeDtypeStruct((rows, 4 * wide + 3 * ff), BF16),
            jax.ShapeDtypeStruct((16, 256), BF16),
        ),
    )(w_out, w_qkv, w_gate_up, w_down, gain_attn, gain_mlp)


def finish(out, dx, grad, gain_grads, wide, ff):
    n, _, length = out.shape
    rows = grad.shape[0]

    def kernel(out_in, dx_in, grad_in, gain_in, out_ref, dx_ref, qkv_ref, back_ref, gu_ref, down_ref, one_ref, two_ref):
        out_ref[...] = out_in[...]
        dx_ref[...] = dx_in[...].astype(F32)

        @pl.when(pl.program_id(0) == 0)
        def _():
            g = grad_in[...].astype(F32)
            back_ref[...] = g[:, :wide].T
            for k in range(3):
                qkv_ref[k] = g[:, (k + 1) * wide : (k + 2) * wide]
            for k in range(2):
                gu_ref[:, k, :] = g[:, 4 * wide + k * ff : 4 * wide + (k + 1) * ff]
            down_ref[...] = g[:, 4 * wide + 2 * ff :]
            one_ref[...] = gain_in[0, :wide]
            two_ref[...] = gain_in[1, :wide]

    def block(*shape):
        return pl.BlockSpec(shape, lambda i: (0,) * len(shape))

    tokens = pl.BlockSpec((1, wide, length), lambda i: (i, 0, 0))
    shapes = ((3, rows, wide), (wide, rows), (rows, 2, ff), (rows, ff), (wide,), (wide,))
    return pl.pallas_call(
        kernel,
        grid=(n,),
        out_shape=(
            jax.ShapeDtypeStruct(out.shape, BF16),
            jax.ShapeDtypeStruct(out.shape, F32),
            *(jax.ShapeDtypeStruct(shape, F32) for shape in shapes),
        ),
        in_specs=[tokens, tokens, block(*grad.shape), block(*gain_grads.shape)],
        out_specs=(tokens, tokens, *(block(*shape) for shape in shapes)),
        compiler_params=pltpu.CompilerParams(vmem_limit_bytes=60 * 2**20),
    )(out, dx, grad, gain_grads)


def solution(mesh):
    tokens, wide = P(("dp", "col"), "row", None), P("col", None, "row")
    back, gain = P("row", "col"), P("row")
    return jax.shard_map(
        functools.partial(shards, mesh.shape["col"] // 4),
        mesh=mesh,
        in_specs=(tokens, P(("dp", "col")), wide, back, wide, back, gain, gain, tokens),
        out_specs=(tokens, tokens, wide, back, wide, back, gain, gain),
        check_vma=False,
    )
```
